32 devices in a mesh: lat: 8 (over z, x), lev: 4 (over y, core).
Axes of the slice: x: 2, y: 2, z: 4, core: 2. Of those that a mesh axis runs over, the one named last changes fastest.
Arguments:
- fields: float32 [4, 128, 32, 512], P(None, 'lev', 'lat'), may hold values from -6 to 6
- courant_lon: float32 [128, 32, 512], P('lev', 'lat'), may hold values from -0.45 to 0.45
- courant_lat: float32 [128, 32, 512], P('lev', 'lat'), may hold values from -0.45 to 0.45
- displacement: float32 [128, 32, 512], P('lev', 'lat'), may hold values from 0 to 0.6
- own_slot: int32 [4, 8, 2], P('lev', 'lat'), may hold values from 0 to 4, as said below
- lent_slot: int32 [4, 8, 2], P('lev', 'lat'), may hold values from 0 to 4, as said below
- w_first: bfloat16 [512, 768], replicated, may hold values from -0.25 to 0.25
- bias_first: float32 [768], replicated, may hold values from -3 to 3
- w_second: bfloat16 [768, 640], replicated, may hold values from -0.21875 to 0.21875
- bias_second: float32 [640], replicated, may hold values from -3 to 3
- w_third: bfloat16 [640, 512], replicated, may hold values from -0.25 to 0.25
- bias_third: float32 [512], replicated, may hold values from -3 to 3
Outputs:
- columns_out: float32 [512, 32, 512], P(None, 'lat', 'lev')
The draws below stay inside these ranges and needn't reach their ends.
Inputs may be any that keep to these rules, and one draw needn't show every extreme that they name: own_slot[g, i, s] is a block of band i and group g (0 to 3) handled in work slot s of that band, or 4 when the slot takes no own block; own blocks fill the first slots. lent_slot[g, i, s] is a block of band i and group g handled in work slot s of band (i + 4) mod 8 of group g, or 4; that slot then holds no own block there; no block appears twice in the two lists of its band and group.
All inputs are finite; a program needn't handle non-finite values.
Results may differ from the reference program's by a relative error of at most 0.002.
Values may be sent and summed in bfloat16 or wider, within the bound.
No kernel may reach another device: no remote copies, remote signals or barrier semaphores. Data moves between devices by JAX's collectives and lax.ppermute only.
A program may use at most 64 MiB of HBM per device.

```python
import jax
import jax.numpy as jnp
from jax import lax

F = 4
LEV = 128
H1 = 768
H2 = 640
BLOCK = 128
LAT_DEV = 4
LON_DEV = 128
IN = 512
BANDS = 8
GROUPS = 4
LAT = 32
LON = 512
BLK_DEV = 4
WORK = 2


def slot_plan(key):
    base_key = jax.random.fold_in(key, 11)
    key_list = jax.random.split(base_key, 4)
    half_bands = BANDS // 2
    first_count = jax.random.randint(key_list[0], (GROUPS, half_bands), 0, BLK_DEV + 1)
    second_count = jax.random.randint(key_list[1], (GROUPS, half_bands), 0, BLK_DEV + 1) % (BLK_DEV - first_count + 1)
    flip_pair = jax.random.randint(key_list[2], (GROUPS, half_bands), 0, 2)
    live_count = jnp.concatenate([jnp.where(flip_pair == 1, second_count, first_count), jnp.where(flip_pair == 1, first_count, second_count)], axis=1)
    rank_scores = jax.random.randint(key_list[3], (GROUPS, BANDS, BLK_DEV), 0, 1 << 20) * BLK_DEV + jnp.arange(BLK_DEV, dtype=jnp.int32)
    block_order = jnp.argsort(rank_scores, axis=-1).astype(jnp.int32)
    slot_index = jnp.arange(WORK, dtype=jnp.int32)
    kept_count = jnp.minimum(live_count, WORK)
    extra_count = jnp.maximum(live_count - WORK, 0)
    own_list = jnp.where(slot_index < kept_count[..., None], block_order[..., :WORK], BLK_DEV)
    partner_count = jnp.roll(live_count, -half_bands, axis=1)
    slot_offset = slot_index - jnp.minimum(partner_count, WORK)[..., None]
    lent_valid = (slot_offset >= 0) & (slot_offset < extra_count[..., None])
    pick_index = jnp.clip(WORK + slot_offset, 0, BLK_DEV - 1).astype(jnp.int32)
    lent_block = jnp.take_along_axis(block_order, pick_index, axis=-1)
    lent_list = jnp.where(lent_valid, lent_block, BLK_DEV)
    return (own_list.astype(jnp.int32), lent_list.astype(jnp.int32))


def draw_own_slot(key, part):
    return slot_plan(key)[0]


def draw_lent_slot(key, part):
    return slot_plan(key)[1]


def block_scale(own_key, extent, shards, least, largest):
    level = 1.0
    for position, parts in shards:
        steps = jax.random.uniform(jax.random.fold_in(jax.random.fold_in(own_key, 6), position), (parts,), jnp.float32, least / len(shards), largest / len(shards))
        level = level * jnp.repeat(jnp.exp(steps), extent[position] // parts).reshape((-1,) + (1,) * (len(extent) - 1 - position))
    return level


def scatter_about(stream_key, shape, spread, most, shards=(), kind=jnp.bfloat16):
    array = jax.random.normal(stream_key, shape, jnp.float32) * spread
    if len(shards) > 0:
        array = block_scale(stream_key, shape, shards, -0.22, 0.18) * array
    return jnp.clip(array, min=-most, max=most).astype(kind)


def setup_inputs(seed: int = 0) -> dict:
    keys = jax.random.split(jax.random.key(seed), 13)
    return {
        "fields": scatter_about(keys[0], (F, LEV, LAT, LON), 1.0, 6.0, ((1, 4), (2, 8)), jnp.float32),
        "courant_lon": jnp.clip(jax.random.uniform(keys[1], (LEV, LAT, LON), jnp.float32, -0.45, 0.45) * block_scale(keys[1], (LEV, LAT, LON), ((0, 4), (1, 8)), -0.4, 0.0), -0.45, 0.45),
        "courant_lat": jnp.clip(jax.random.uniform(keys[2], (LEV, LAT, LON), jnp.float32, -0.45, 0.45) * block_scale(keys[2], (LEV, LAT, LON), ((0, 4), (1, 8)), -0.4, 0.0), -0.45, 0.45),
        "displacement": jnp.clip(0.6 * jax.random.uniform(keys[3], (LEV, LAT, LON), jnp.float32) ** block_scale(keys[3], (LEV, LAT, LON), ((0, 4), (1, 8)), -0.2, 0.2), 0.0, 0.6),
        "own_slot": draw_own_slot(jax.random.fold_in(keys[12], 71), 0),
        "lent_slot": draw_lent_slot(jax.random.fold_in(keys[12], 71), 0),
        "w_first": scatter_about(keys[6], (IN, H1), IN ** -0.5, 0.25),
        "bias_first": scatter_about(keys[7], (H1,), 0.5, 3.0, (), jnp.float32),
        "w_second": scatter_about(keys[8], (H1, H2), H1 ** -0.5, 0.21875),
        "bias_second": scatter_about(keys[9], (H2,), 0.5, 3.0, (), jnp.float32),
        "w_third": scatter_about(keys[10], (H2, IN), H2 ** -0.5, 0.25),
        "bias_third": scatter_about(keys[11], (IN,), 0.5, 3.0, (), jnp.float32),
    }


def upwind(fields, western, eastern, northern, southern, along_lon, along_lat):
    result = fields - jnp.maximum(along_lon, 0.0) * (fields - western)
    result = result - jnp.minimum(along_lon, 0.0) * (eastern - fields)
    result = result - jnp.maximum(along_lat, 0.0) * (fields - northern)
    return result - jnp.minimum(along_lat, 0.0) * (southern - fields)


def network(rows, w_first, bias_first, w_second, bias_second, w_third, bias_third):
    hidden = jnp.dot(rows, w_first, preferred_element_type=jnp.float32) + bias_first
    hidden = jax.nn.silu(hidden).astype(jnp.bfloat16)
    hidden = jnp.dot(hidden, w_second, preferred_element_type=jnp.float32) + bias_second
    hidden = jax.nn.silu(hidden).astype(jnp.bfloat16)
    return (jnp.dot(hidden, w_third, preferred_element_type=jnp.float32) + bias_third).astype(jnp.bfloat16)


def reference(fields, courant_lon, courant_lat, displacement, own_slot, lent_slot, w_first, bias_first, w_second, bias_second, w_third, bias_third):
    padded = jnp.pad(fields, ((0, 0), (0, 0), (1, 1), (0, 0)))
    advected = upwind(fields, jnp.roll(fields, 1, axis=3), jnp.roll(fields, -1, axis=3), padded[:, :, :-2, :], padded[:, :, 2:, :], courant_lon[None], courant_lat[None])
    depth = lax.broadcasted_iota(jnp.int32, (1, LEV, 1, 1), 1)
    flux = jnp.where(depth < LEV - 1, displacement[None] * advected, 0.0)
    above = jnp.concatenate([jnp.zeros_like(flux[:, :1]), flux[:, :-1]], axis=1)
    remapped = advected - flux + above
    width = F * LEV
    columns = jnp.transpose(remapped, (2, 3, 0, 1)).reshape(LAT, LON, width)
    blocks = columns.reshape(BANDS, LAT_DEV, GROUPS, LON_DEV, width).transpose(2, 0, 1, 3, 4).reshape(GROUPS, BANDS, BLK_DEV, BLOCK, width)
    inputs = blocks.astype(jnp.bfloat16)
    own_safe = jnp.minimum(own_slot, BLK_DEV - 1).astype(jnp.int32)
    lent_safe = jnp.minimum(lent_slot, BLK_DEV - 1).astype(jnp.int32)
    own_rows = jnp.take_along_axis(inputs, own_safe[:, :, :, None, None], axis=2)
    lent_rows = jnp.take_along_axis(inputs, lent_safe[:, :, :, None, None], axis=2)
    lent_rows = jnp.where((lent_slot < BLK_DEV)[:, :, :, None, None], lent_rows, jnp.zeros_like(lent_rows))
    arrived = jnp.roll(lent_rows, -(BANDS // 2), axis=1)
    work_rows = jnp.where((own_slot < BLK_DEV)[:, :, :, None, None], own_rows, arrived)

    def per_group(group_rows):
        flat = network(group_rows.reshape(-1, width), w_first, bias_first, w_second, bias_second, w_third, bias_third)
        return flat.reshape(group_rows.shape)

    tendency = lax.map(per_group, work_rows)
    returned = jnp.roll(tendency, -(BANDS // 2), axis=1)
    block_ids = lax.broadcasted_iota(jnp.int32, (1, 1, BLK_DEV, 1, 1), 2)
    added = jnp.zeros(blocks.shape, jnp.float32)
    for slot_number in range(WORK):
        own_hit = own_slot[:, :, slot_number][:, :, None, None, None] == block_ids
        lent_hit = lent_slot[:, :, slot_number][:, :, None, None, None] == block_ids
        added = added + jnp.where(own_hit, tendency[:, :, slot_number][:, :, None].astype(jnp.float32), 0.0)
        added = added + jnp.where(lent_hit, returned[:, :, slot_number][:, :, None].astype(jnp.float32), 0.0)
    result = blocks + added
    return result.reshape(GROUPS, BANDS, LAT_DEV, LON_DEV, width).transpose(4, 1, 2, 0, 3).reshape(width, LAT, LON)
```

```python
import functools

import jax
import jax.numpy as jnp
from jax import lax
from jax.experimental import pallas as pl
from jax.experimental.pallas import tpu as pltpu
from jax.sharding import PartitionSpec as P

LANES = 128
SCALE = 4096.0
MEGA = 1024 * 1024
VMEM = pl.BlockSpec(memory_space=pltpu.VMEM)
SMEM = pl.BlockSpec(memory_space=pltpu.SMEM)
ANY = pl.BlockSpec(memory_space=pl.ANY)


def place(me, other, count):
    if count & (count - 1) == 0:
        return lax.bitwise_xor(me, other)
    return lax.rem(other - me + count, count)


def partner(me, step, count):
    if count & (count - 1) == 0:
        return me ^ step
    return (me + step) % count


def source(me, step, count):
    if count & (count - 1) == 0:
        return lax.bitwise_xor(me, step)
    return lax.rem(me - step + count, count)


def exchange(value, step, count):
    return lax.ppermute(value, "lev", [(i, partner(i, step, count)) for i in range(count)])


def params(mega=40):
    return pltpu.CompilerParams(vmem_limit_bytes=mega * MEGA)


def cost(flops, moved):
    return pl.CostEstimate(flops=flops, bytes_accessed=moved, transcendentals=0)


def edge_kernel(fields, out, sem):
    odd = lax.rem(lax.axis_index("lat"), 2)
    last = fields.shape[2] - 1
    copies = [
        pltpu.make_async_copy(fields.at[:, :, 0, :], out.at[1 - odd], sem.at[0]),
        pltpu.make_async_copy(fields.at[:, :, last, :], out.at[odd], sem.at[1]),
    ]
    for copy in copies:
        copy.start()
    for copy in copies:
        copy.wait()


def edge_rows(fields):
    count, levels, _, lon = fields.shape
    return pl.pallas_call(
        edge_kernel,
        in_specs=[ANY],
        out_specs=VMEM,
        out_shape=jax.ShapeDtypeStruct((2, count, levels, lon), fields.dtype),
        scratch_shapes=[pltpu.SemaphoreType.DMA((2,))],
        compiler_params=params(),
        name="edge_rows",
    )(fields)


def store_message(message, at, field, fields_count, advected, share, groups, me):
    levels = advected.shape[0]
    flux = share * advected
    depth = lax.broadcasted_iota(jnp.int32, flux.shape, 0)
    above = jnp.where(depth == 0, 0.0, pltpu.roll(flux, 1, 0))
    remapped = advected - flux + above
    base = field * levels
    for group in range(groups):
        where = place(me, group, groups)
        lanes = slice(group * LANES, (group + 1) * LANES)
        spot = (where,) + at
        message[spot + (slice(base, base + levels), slice(None))] = remapped[:, lanes]
        row = fields_count * levels + field
        message[spot + (slice(row, row + 1), slice(None))] = flux[levels - 1 :, lanes]


def advect_kernel(
    groups, fields, along_lon, along_lat, displacement, edges,
    message, partial, weight, share, inner, lon_row, lat_row, moved_row, sem,
):
    count, levels, rows, lon = fields.shape
    odd = lax.rem(lax.axis_index("lat"), 2)
    me = lax.axis_index("lev")
    copies = []
    for row in range(rows):
        copies.append(pltpu.make_async_copy(along_lon.at[:, row, :], lon_row.at[row], sem.at[0, row]))
        copies.append(pltpu.make_async_copy(along_lat.at[:, row, :], lat_row.at[row], sem.at[1, row]))
        copies.append(pltpu.make_async_copy(displacement.at[:, row, :], moved_row.at[row], sem.at[2, row]))
        if 0 < row < rows - 1:
            copies.append(pltpu.make_async_copy(fields.at[:, :, row, :], inner.at[row - 1], sem.at[3, row]))
    for copy in copies:
        copy.start()
    for copy in copies:
        copy.wait()
    depth = lax.broadcasted_iota(jnp.int32, (levels, lon), 0)
    bottom = jnp.logical_and(depth == levels - 1, me == groups - 1)

    def line(row, field):
        if row == 0:
            return edges[1 - odd, field]
        if row == rows - 1:
            return edges[odd, field]
        return inner[row - 1, field]

    for row in range(rows):
        c_lon = lon_row[row]
        c_lat = lat_row[row]
        east_wind, west_wind = jnp.maximum(c_lon, 0.0), jnp.minimum(c_lon, 0.0)
        south_wind, north_wind = jnp.maximum(c_lat, 0.0), jnp.minimum(c_lat, 0.0)
        moved = jnp.where(bottom, 0.0, moved_row[row])
        slot = 1 - odd if row == 0 else odd
        if row == 0:
            weight[slot] = south_wind
            share[slot] = moved
        elif row == rows - 1:
            weight[slot] = -north_wind
            share[slot] = moved
        for field in range(count):
            here = line(row, field)
            result = here - east_wind * (here - pltpu.roll(here, 1, 1))
            result = result - west_wind * (pltpu.roll(here, lon - 1, 1) - here)
            north = line(row - 1, field) if row > 0 else 0.0
            south = line(row + 1, field) if row < rows - 1 else 0.0
            result = result - south_wind * (here - north)
            result = result - north_wind * (south - here)
            if 0 < row < rows - 1:
                store_message(message, (row - 1,), field, count, result, moved, groups, me)
            else:
                partial[slot, field] = result


def padded_height(count, levels):
    return -(-(count * levels + count) // 16) * 16


def advect(fields, along_lon, along_lat, displacement, edges, groups):
    count, levels, rows, lon = fields.shape
    height = padded_height(count, levels)
    f32 = jnp.float32
    return pl.pallas_call(
        functools.partial(advect_kernel, groups),
        in_specs=[ANY, ANY, ANY, ANY, VMEM],
        out_specs=[VMEM] * 4,
        out_shape=[
            jax.ShapeDtypeStruct((groups, rows - 2, height, LANES), f32),
            jax.ShapeDtypeStruct((2, count, levels, lon), f32),
            jax.ShapeDtypeStruct((2, levels, lon), f32),
            jax.ShapeDtypeStruct((2, levels, lon), f32),
        ],
        scratch_shapes=[
            pltpu.VMEM((rows - 2, count, levels, lon), f32),
            pltpu.VMEM((rows, levels, lon), f32),
            pltpu.VMEM((rows, levels, lon), f32),
            pltpu.VMEM((rows, levels, lon), f32),
            pltpu.SemaphoreType.DMA((4, rows)),
        ],
        compiler_params=params(),
        cost_estimate=cost(2_000_000_000, 6_000_000),
        name="advect",
    )(fields, along_lon, along_lat, displacement, edges)


def finish_kernel(groups, slot, partial, weight, share, halo, message):
    count = partial.shape[1]
    me = lax.axis_index("lev")
    wind, moved = weight[slot], share[slot]
    for field in range(count):
        advected = partial[slot, field] + wind * halo[field]
        store_message(message, (), field, count, advected, moved, groups, me)


def finish(partial, weight, share, halo, groups, slot):
    _, count, levels, _ = partial.shape
    return pl.pallas_call(
        functools.partial(finish_kernel, groups, slot),
        in_specs=[VMEM] * 4,
        out_specs=VMEM,
        out_shape=jax.ShapeDtypeStruct((groups, padded_height(count, levels), LANES), jnp.float32),
        compiler_params=params(),
        name="finish",
    )(partial, weight, share, halo)


def turn_kernel(first, second, third, first_out, second_out, third_out):
    first_out[...] = first[...].T
    second_out[...] = second[...].T
    third_out[...] = third[...].T


def turned(first, second, third):
    return pl.pallas_call(
        turn_kernel,
        in_specs=[VMEM] * 3,
        out_specs=[VMEM] * 3,
        out_shape=[jax.ShapeDtypeStruct(w.shape[::-1], w.dtype) for w in (first, second, third)],
        compiler_params=params(),
        cost_estimate=cost(2_000_000_000, 5_000_000),
        name="turned",
    )(first, second, third)


def silu(value):
    half = 0.5 * value
    return half + half * jnp.tanh(half)


def physics_kernel(groups, blocks, count, levels, aliased, *refs):
    parts, refs = refs[:groups], refs[groups:]
    own, lent, first, bias_first, second, bias_second, third, bias_third = refs[:8]
    refs = refs[8 + aliased :]
    out, columns, carried, staged, sem = refs
    me = lax.axis_index("lev")
    odd = lax.rem(lax.axis_index("lat"), 2)
    depth = groups * levels
    many = len(blocks)
    for index in range(many):
        for step in range(groups):
            level = source(me, step, groups)
            part = parts[step]
            for field in range(count):
                start = pl.multiple_of(field * depth + level * levels, levels)
                columns[index, pl.ds(start, levels), :] = part[index, field * levels : (field + 1) * levels, :]
            carried[index, level, 0:count, :] = part[index, count * levels : count * levels + count, :]
        for field in range(count):
            for level in range(1, groups):
                row = field * depth + level * levels
                columns[index, row : row + 1, :] += carried[index, level - 1, field : field + 1, :]
    value = jnp.concatenate([columns[index].astype(jnp.bfloat16) for index in range(many)], axis=1)
    hidden = jnp.dot(first[...], value, preferred_element_type=jnp.float32) + bias_first[...]
    hidden = silu(hidden).astype(jnp.bfloat16)
    hidden = jnp.dot(second[...], hidden, preferred_element_type=jnp.float32) + bias_second[...]
    hidden = silu(hidden).astype(jnp.bfloat16)
    tendency = jnp.dot(third[...], hidden, preferred_element_type=jnp.float32) + bias_third[...]
    tendency = tendency.astype(jnp.bfloat16).astype(jnp.float32)
    slots = own.shape[-1]
    for index in range(many):
        block = blocks[index]
        number = block if isinstance(block, int) else jnp.where(odd == 1, block[1], block[0])
        active = own[0, 0, 0] == number
        for slot in range(slots):
            active = jnp.logical_or(active, own[0, 0, slot] == number)
            active = jnp.logical_or(active, lent[0, 0, slot] == number)
        part = tendency[:, index * LANES : (index + 1) * LANES]
        staged[index] = columns[index] + jnp.where(active, part, 0.0)

    for index in range(many):
        block = blocks[index]
        if isinstance(block, int):
            pltpu.make_async_copy(staged.at[index], out.at[:, block, :], sem.at[index]).start()
        else:
            for parity in range(2):

                @pl.when(odd == parity)
                def _():
                    pltpu.make_async_copy(staged.at[index], out.at[:, block[parity], :], sem.at[index]).start()

    for index in range(many):
        block = blocks[index]
        row = block if isinstance(block, int) else 0
        pltpu.make_async_copy(staged.at[index], out.at[:, row, :], sem.at[index]).wait()


def physics(parts, own, lent, network, rows, blocks, count, levels, result=None):
    groups = len(parts)
    many = len(blocks)
    width = count * groups * levels
    f32 = jnp.float32
    aliased = 0 if result is None else 1
    operands = [*parts, own, lent, *network]
    specs = [VMEM] * groups + [SMEM, SMEM] + [VMEM] * 6
    if aliased:
        operands.append(result)
        specs.append(ANY)
    return pl.pallas_call(
        functools.partial(physics_kernel, groups, blocks, count, levels, aliased),
        in_specs=specs,
        out_specs=ANY,
        out_shape=jax.ShapeDtypeStruct((width, rows, LANES), f32),
        scratch_shapes=[
            pltpu.VMEM((many, width, LANES), f32),
            pltpu.VMEM((many, groups, 8, LANES), f32),
            pltpu.VMEM((many, width, LANES), f32),
            pltpu.SemaphoreType.DMA((many,)),
        ],
        input_output_aliases={len(operands) - 1: 0} if aliased else {},
        compiler_params=params(),
        cost_estimate=cost(2_000_000_000, 5_000_000),
        name="physics",
    )(*operands)


def body(
    fields,
    courant_lon,
    courant_lat,
    displacement,
    own_slot,
    lent_slot,
    w_first,
    bias_first,
    w_second,
    bias_second,
    w_third,
    bias_third,
):
    count, levels, rows, lon = fields.shape
    groups = lax.axis_size("lev")
    bands = lax.axis_size("lat")
    half = jnp.float16
    f32 = jnp.float32

    edges = edge_rows(fields)
    near_pairs = [(i, i ^ 1) for i in range(bands) if i ^ 1 < bands]
    far_pairs = [(i, i + 1 if i % 2 else i - 1) for i in range(bands)]
    far_pairs = [(i, j) for i, j in far_pairs if 0 <= j < bands]
    near = lax.ppermute((edges[0] * SCALE).astype(half), "lat", near_pairs)
    far = lax.ppermute((edges[1] * SCALE).astype(half), "lat", far_pairs)
    message, partial, weight, share = advect(fields, courant_lon, courant_lat, displacement, edges, groups)
    weights = turned(w_first, w_second, w_third)
    biases = [b.reshape(-1, 1) for b in (bias_first, bias_second, bias_third)]
    network = [x for pair in zip(weights, biases) for x in pair]

    def swap(own_first):
        parts = [own_first[0]]
        for step in range(1, groups):
            sent = exchange((own_first[step] * SCALE).astype(half), step, groups)
            parts.append(sent.astype(f32) * (1.0 / SCALE))
        return parts

    near_message = finish(partial, weight, share, near.astype(f32) * (1.0 / SCALE), groups, 0)
    early = swap(jnp.concatenate([message, near_message[:, None]], axis=1))
    far_message = finish(partial, weight, share, far.astype(f32) * (1.0 / SCALE), groups, 1)
    late = swap(far_message[:, None])
    inner = tuple(range(1, rows - 1))
    result = physics(early, own_slot, lent_slot, network, rows, inner + ((rows - 1, 0),), count, levels)
    return physics(late, own_slot, lent_slot, network, rows, ((0, rows - 1),), count, levels, result)


def solution(mesh):
    in_specs = (
        P(None, "lev", "lat", None),
        P("lev", "lat", None),
        P("lev", "lat", None),
        P("lev", "lat", None),
        P("lev", "lat", None),
        P("lev", "lat", None),
        P(),
        P(),
        P(),
        P(),
        P(),
        P(),
    )
    out_specs = P(None, "lat", "lev")
    return jax.shard_map(body, mesh=mesh, in_specs=in_specs, out_specs=out_specs, check_vma=False)
```

```python
import functools

import jax
import jax.numpy as jnp
from jax import lax
from jax.experimental import pallas as pl
from jax.experimental.pallas import tpu as pltpu
from jax.sharding import PartitionSpec as P

LANES = 128
SCALE = 4096.0
MEGA = 1024 * 1024
VMEM = pl.BlockSpec(memory_space=pltpu.VMEM)
ANY = pl.BlockSpec(memory_space=pl.ANY)


def place(me, other, count):
    if count & (count - 1) == 0:
        return lax.bitwise_xor(me, other)
    return lax.rem(other - me + count, count)


def source(me, step, count):
    if count & (count - 1) == 0:
        return lax.bitwise_xor(me, step)
    return lax.rem(me - step + count, count)


def exchange(value, step, count):
    power = count & (count - 1) == 0
    return lax.ppermute(value, "lev", [(i, i ^ step if power else (i + step) % count) for i in range(count)])


def params(mega=16):
    return pltpu.CompilerParams(vmem_limit_bytes=mega * MEGA)


def cost(flops, moved):
    return pl.CostEstimate(flops=flops, bytes_accessed=moved, transcendentals=0)


def edge_kernel(fields, out):
    out[0] = fields[:, :, 0, :]
    out[1] = fields[:, :, fields.shape[2] - 1, :]


def edge_rows(fields):
    count, levels, _, lon = fields.shape
    return pl.pallas_call(
        edge_kernel,
        in_specs=[VMEM],
        out_specs=VMEM,
        out_shape=jax.ShapeDtypeStruct((2, count, levels, lon), fields.dtype),
        compiler_params=params(),
        name="edge_rows",
    )(fields)


def message_height(rows, count, levels):
    return rows * count * levels + -(-rows * count // 8) * 8


def store_message(message, index, rows, field, count, advected, share, groups, me):
    levels = advected.shape[0]
    flux = share * advected
    depth = lax.broadcasted_iota(jnp.int32, flux.shape, 0)
    above = jnp.where(depth == 0, 0.0, pltpu.roll(flux, 1, 0))
    remapped = advected - flux + above
    base = (index * count + field) * levels
    row = rows * count * levels + index * count + field
    for group in range(groups):
        where = place(me, group, groups)
        lanes = slice(group * LANES, (group + 1) * LANES)
        message[where, base : base + levels, :] = remapped[:, lanes]
        message[where, row : row + 1, :] = flux[levels - 1 :, lanes]


def moved_share(displacement, row, me, groups):
    share = displacement[:, row, :]
    depth = lax.broadcasted_iota(jnp.int32, share.shape, 0)
    bottom = jnp.logical_and(depth == share.shape[0] - 1, me == groups - 1)
    return jnp.where(bottom, 0.0, share)


def winds(courant):
    return jnp.maximum(courant, 0.0), jnp.minimum(courant, 0.0)


def along_row(here, east_wind, west_wind):
    lon = here.shape[-1]
    result = here - east_wind * (here - pltpu.roll(here, 1, 1))
    return result - west_wind * (pltpu.roll(here, lon - 1, 1) - here)


def inner_kernel(groups, fields, along_lon, along_lat, displacement, edges, message):
    count, _, rows, _ = fields.shape
    me = lax.axis_index("lev")
    for row in range(1, rows - 1):
        east_wind, west_wind = winds(along_lon[:, row, :])
        south_wind, north_wind = winds(along_lat[:, row, :])
        share = moved_share(displacement, row, me, groups)
        for field in range(count):
            here = fields[field, :, row, :]
            north = edges[0, field] if row == 1 else fields[field, :, row - 1, :]
            south = edges[1, field] if row == rows - 2 else fields[field, :, row + 1, :]
            result = along_row(here, east_wind, west_wind)
            result = result - south_wind * (here - north)
            result = result - north_wind * (south - here)
            store_message(message, row - 1, rows - 2, field, count, result, share, groups, me)


def inner_rows(fields, along_lon, along_lat, displacement, edges, groups):
    count, levels, rows, _ = fields.shape
    height = message_height(rows - 2, count, levels)
    return pl.pallas_call(
        functools.partial(inner_kernel, groups),
        in_specs=[VMEM] * 5,
        out_specs=VMEM,
        out_shape=jax.ShapeDtypeStruct((groups, height, LANES), jnp.float32),
        compiler_params=params(),
        cost_estimate=cost(1_000_000_000, 3_000_000),
        name="inner_rows",
    )(fields, along_lon, along_lat, displacement, edges)


def outer_kernel(groups, fields, along_lon, along_lat, displacement, edges, partial, weight, share):
    count, _, rows, _ = fields.shape
    me = lax.axis_index("lev")
    for index, row in enumerate((0, rows - 1)):
        east_wind, west_wind = winds(along_lon[:, row, :])
        south_wind, north_wind = winds(along_lat[:, row, :])
        weight[index] = south_wind if index == 0 else -north_wind
        share[index] = moved_share(displacement, row, me, groups)
        for field in range(count):
            here = edges[index, field]
            north = fields[field, :, row - 1, :] if index else 0.0
            south = 0.0 if index else fields[field, :, row + 1, :]
            result = along_row(here, east_wind, west_wind)
            result = result - south_wind * (here - north)
            partial[index, field] = result - north_wind * (south - here)


def outer_rows(fields, along_lon, along_lat, displacement, edges, groups):
    count, levels, _, lon = fields.shape
    f32 = jnp.float32
    return pl.pallas_call(
        functools.partial(outer_kernel, groups),
        in_specs=[VMEM] * 5,
        out_specs=[VMEM] * 3,
        out_shape=[
            jax.ShapeDtypeStruct((2, count, levels, lon), f32),
            jax.ShapeDtypeStruct((2, levels, lon), f32),
            jax.ShapeDtypeStruct((2, levels, lon), f32),
        ],
        compiler_params=params(),
        cost_estimate=cost(1_000_000_000, 3_000_000),
        name="outer_rows",
    )(fields, along_lon, along_lat, displacement, edges)


def finish_kernel(groups, partial, weight, share, north, south, _, message, unit):
    unit[...] = jnp.full(unit.shape, 1.0 / SCALE, jnp.float32)
    count = partial.shape[1]
    me = lax.axis_index("lev")
    for index, halo in enumerate((north, south)):
        wind, moved = weight[index], share[index]
        for field in range(count):
            advected = partial[index, field] + wind * halo[field]
            store_message(message, index, 2, field, count, advected, moved, groups, me)


def finish(partial, weight, share, north, south, after, groups):
    _, count, levels, _ = partial.shape
    return pl.pallas_call(
        functools.partial(finish_kernel, groups),
        in_specs=[VMEM] * 5 + [ANY],
        out_specs=[VMEM] * 2,
        out_shape=[
            jax.ShapeDtypeStruct((groups, message_height(2, count, levels), LANES), jnp.float32),
            jax.ShapeDtypeStruct((8, LANES), jnp.float32),
        ],
        compiler_params=params(),
        name="finish",
    )(partial, weight, share, north, south, after)


def turn_kernel(rows, _, own, lent, first, second, third, bias_first, bias_second, bias_third, *outs):
    for weight, out in zip((first, second, third), outs[:3]):
        out[...] = weight[...].T
    for bias, out in zip((bias_first, bias_second, bias_third), outs[3:6]):
        out[...] = jnp.broadcast_to(bias[...][None, :], (8, bias.shape[0])).T
    for row in range(rows):
        hits = jnp.logical_or(own[0] == row, lent[0] == row)
        active = jnp.max(jnp.where(hits, 1.0, 0.0), axis=1, keepdims=True)
        outs[6][row] = jnp.broadcast_to(active, (8, LANES))


def turned(after, own, lent, weights, biases, rows):
    f32 = jnp.float32
    shapes = [jax.ShapeDtypeStruct(w.shape[::-1], w.dtype) for w in weights]
    shapes += [jax.ShapeDtypeStruct((b.shape[0], 8), f32) for b in biases]
    shapes += [jax.ShapeDtypeStruct((rows, 8, LANES), f32)]
    return pl.pallas_call(
        functools.partial(turn_kernel, rows),
        in_specs=[ANY] + [VMEM] * 8,
        out_specs=[VMEM] * 7,
        out_shape=shapes,
        compiler_params=params(),
        cost_estimate=cost(1_000_000_000, 5_000_000),
        name="turned",
    )(after, own, lent, *weights, *biases)


def silu(value):
    half = 0.5 * value
    return half + half * jnp.tanh(half)


def layer(weight, bias, value, act):
    parts = []
    for start in range(0, weight.shape[0], 256):
        stop = min(start + 256, weight.shape[0])
        total = jnp.dot(weight[start:stop, :], value, preferred_element_type=jnp.float32)
        parts.append(act(total + bias[start:stop, 0:1]).astype(jnp.bfloat16))
    return jnp.concatenate(parts, axis=0)


def physics_kernel(groups, blocks, count, levels, aliased, *refs):
    parts, refs = refs[:groups], refs[groups:]
    first, second, third, bias_first, bias_second, bias_third, mask = refs[:7]
    out, columns, carried, staged, sem = refs[7 + aliased :]
    me = lax.axis_index("lev")
    depth = groups * levels
    many = len(blocks)
    tall = many * count * levels
    for step in range(groups):
        level = source(me, step, groups)
        part = parts[step]
        for index in range(many):
            for field in range(count):
                start = pl.multiple_of(field * depth + level * levels, levels)
                base = (index * count + field) * levels
                columns[index, pl.ds(start, levels), :] = part[base : base + levels, :]
        carried[level, 0 : many * count, :] = part[tall : tall + many * count, :]
    for index in range(many):
        for field in range(count):
            for level in range(1, groups):
                row = field * depth + level * levels
                line = index * count + field
                columns[index, row : row + 1, :] += carried[level - 1, line : line + 1, :]
    value = jnp.concatenate([columns[index].astype(jnp.bfloat16) for index in range(many)], axis=1)
    hidden = layer(first, bias_first, value, silu)
    hidden = layer(second, bias_second, hidden, silu)
    tendency = layer(third, bias_third, hidden, lambda v: v).astype(jnp.float32)
    copies = []
    for index, block in enumerate(blocks):
        part = tendency[:, index * LANES : (index + 1) * LANES]
        staged[index] = columns[index] + jnp.where(mask[block, 0:1, :] > 0.0, part, 0.0)
        copies.append(pltpu.make_async_copy(staged.at[index], out.at[:, block, :], sem.at[index]))
        copies[-1].start()
    for copy in copies:
        copy.wait()


def physics(parts, network, rows, blocks, count, levels, result=None):
    groups = len(parts)
    many = len(blocks)
    width = count * groups * levels
    f32 = jnp.float32
    aliased = result is not None
    operands = [*parts, *network]
    specs = [VMEM] * len(operands)
    if aliased:
        operands.append(result)
        specs.append(ANY)
    return pl.pallas_call(
        functools.partial(physics_kernel, groups, blocks, count, levels, int(aliased)),
        in_specs=specs,
        out_specs=ANY,
        out_shape=jax.ShapeDtypeStruct((width, rows, LANES), f32),
        scratch_shapes=[
            pltpu.VMEM((many, width, LANES), f32),
            pltpu.VMEM((groups, -(-many * count // 8) * 8, LANES), f32),
            pltpu.VMEM((many, width, LANES), f32),
            pltpu.SemaphoreType.DMA((many,)),
        ],
        input_output_aliases={len(operands) - 1: 0} if aliased else {},
        compiler_params=params(),
        cost_estimate=cost(20_000_000_000, 5_000_000),
        name="physics",
    )(*operands)


def body(
    fields,
    courant_lon,
    courant_lat,
    displacement,
    own_slot,
    lent_slot,
    w_first,
    bias_first,
    w_second,
    bias_second,
    w_third,
    bias_third,
):
    count, levels, rows, lon = fields.shape
    groups = lax.axis_size("lev")
    bands = lax.axis_size("lat")
    even = lax.axis_index("lat") % 2 == 0
    half = jnp.float16
    f32 = jnp.float32

    near_pairs = [(i, i ^ 1) for i in range(bands) if i ^ 1 < bands]
    far_pairs = [(i, i + 1 if i % 2 else i - 1) for i in range(bands)]
    far_pairs = [(i, j) for i, j in far_pairs if 0 <= j < bands]
    edges = edge_rows(fields)
    far = lax.ppermute((jnp.where(even, edges[0], edges[1]) * SCALE).astype(half), "lat", far_pairs)
    near = lax.ppermute((jnp.where(even, edges[1], edges[0]) * SCALE).astype(half), "lat", near_pairs)

    def swap(message):
        sent = [(message[step] * SCALE).astype(half) for step in range(1, groups)]
        return [exchange(value, step + 1, groups) for step, value in enumerate(sent)]

    def received(message, values, unit):
        return [message[0]] + [value.astype(f32) * unit[0:1, :] for value in values]

    inner = inner_rows(fields, courant_lon, courant_lat, displacement, edges, groups)
    inner_moved = swap(inner)
    partial, weight, share = outer_rows(fields, courant_lon, courant_lat, displacement, edges, groups)
    weights, biases = (w_first, w_second, w_third), (bias_first, bias_second, bias_third)
    network = turned(inner, own_slot, lent_slot, weights, biases, rows)
    north = jnp.where(even, far, near).astype(f32) * (1.0 / SCALE)
    south = jnp.where(even, near, far).astype(f32) * (1.0 / SCALE)
    outer, unit = finish(partial, weight, share, north, south, network[-1], groups)
    outer_moved = swap(outer)
    result = physics(received(inner, inner_moved, unit), network, rows, tuple(range(1, rows - 1)), count, levels)
    return physics(received(outer, outer_moved, jnp.full((1, LANES), 1.0 / SCALE, f32)), network, rows, (0, rows - 1), count, levels, result)


def solution(mesh):
    in_specs = (
        P(None, "lev", "lat", None),
        P("lev", "lat", None),
        P("lev", "lat", None),
        P("lev", "lat", None),
        P("lev", "lat", None),
        P("lev", "lat", None),
        P(),
        P(),
        P(),
        P(),
        P(),
        P(),
    )
    out_specs = P(None, "lat", "lev")
    return jax.shard_map(body, mesh=mesh, in_specs=in_specs, out_specs=out_specs, check_vma=False)
```

```python
import functools

import jax
import jax.numpy as jnp
from jax import lax
from jax.experimental import pallas as pl
from jax.experimental.pallas import tpu as pltpu
from jax.sharding import PartitionSpec as P

LANES = 128
SCALE = 4096.0
MEGA = 1024 * 1024
VMEM = pl.BlockSpec(memory_space=pltpu.VMEM)
ANY = pl.BlockSpec(memory_space=pl.ANY)


def place(me, other, count):
    if count & (count - 1) == 0:
        return lax.bitwise_xor(me, other)
    return lax.rem(other - me + count, count)


def source(me, step, count):
    if count & (count - 1) == 0:
        return lax.bitwise_xor(me, step)
    return lax.rem(me - step + count, count)


def exchange(value, step, count):
    power = count & (count - 1) == 0
    return lax.ppermute(value, "lev", [(i, i ^ step if power else (i + step) % count) for i in range(count)])


def params(mega=16):
    return pltpu.CompilerParams(vmem_limit_bytes=mega * MEGA)


def cost(flops, moved):
    return pl.CostEstimate(flops=flops, bytes_accessed=moved, transcendentals=0)


def edge_kernel(fields, out):
    out[0] = fields[:, :, 0, :]
    out[1] = fields[:, :, fields.shape[2] - 1, :]


def edge_rows(fields):
    count, levels, _, lon = fields.shape
    return pl.pallas_call(
        edge_kernel,
        in_specs=[VMEM],
        out_specs=VMEM,
        out_shape=jax.ShapeDtypeStruct((2, count, levels, lon), fields.dtype),
        compiler_params=params(),
        name="edge_rows",
    )(fields)


def message_height(rows, count, levels):
    return rows * count * levels + -(-rows * count // 8) * 8


def store_message(message, index, rows, field, count, advected, share, groups, me):
    levels = advected.shape[0]
    flux = share * advected
    depth = lax.broadcasted_iota(jnp.int32, flux.shape, 0)
    above = jnp.where(depth == 0, 0.0, pltpu.roll(flux, 1, 0))
    remapped = advected - flux + above
    base = (index * count + field) * levels
    row = rows * count * levels + index * count + field
    for group in range(groups):
        where = place(me, group, groups)
        lanes = slice(group * LANES, (group + 1) * LANES)
        message[where, base : base + levels, :] = remapped[:, lanes]
        message[where, row : row + 1, :] = flux[levels - 1 :, lanes]


def moved_share(displacement, row, me, groups):
    share = displacement[:, row, :]
    depth = lax.broadcasted_iota(jnp.int32, share.shape, 0)
    bottom = jnp.logical_and(depth == share.shape[0] - 1, me == groups - 1)
    return jnp.where(bottom, 0.0, share)


def winds(courant):
    return jnp.maximum(courant, 0.0), jnp.minimum(courant, 0.0)


def along_row(here, east_wind, west_wind):
    lon = here.shape[-1]
    result = here - east_wind * (here - pltpu.roll(here, 1, 1))
    return result - west_wind * (pltpu.roll(here, lon - 1, 1) - here)


def local_kernel(groups, inner, fields, along_lon, along_lat, displacement, edges, *outs):
    count, _, rows, _ = fields.shape
    me = lax.axis_index("lev")

    def line(row, field):
        return edges[int(row > 0), field] if row in (0, rows - 1) else fields[field, :, row, :]

    for row in range(1, rows - 1) if inner else (0, rows - 1):
        east_wind, west_wind = winds(along_lon[:, row, :])
        south_wind, north_wind = winds(along_lat[:, row, :])
        moved = moved_share(displacement, row, me, groups)
        index = int(row > 0)
        if not inner:
            outs[1][index] = -north_wind if row else south_wind
            outs[2][index] = moved
        for field in range(count):
            here = line(row, field)
            north = line(row - 1, field) if row else 0.0
            south = line(row + 1, field) if row < rows - 1 else 0.0
            result = along_row(here, east_wind, west_wind)
            result = result - south_wind * (here - north)
            result = result - north_wind * (south - here)
            if inner:
                store_message(outs[0], row - 1, rows - 2, field, count, result, moved, groups, me)
            else:
                outs[0][index, field] = result


def local_rows(inner, fields, along_lon, along_lat, displacement, edges, groups):
    count, levels, rows, lon = fields.shape
    f32 = jnp.float32
    shapes = [
        jax.ShapeDtypeStruct((2, count, levels, lon), f32),
        jax.ShapeDtypeStruct((2, levels, lon), f32),
        jax.ShapeDtypeStruct((2, levels, lon), f32),
    ]
    if inner:
        shapes = [jax.ShapeDtypeStruct((groups, message_height(rows - 2, count, levels), LANES), f32)]
    return pl.pallas_call(
        functools.partial(local_kernel, groups, inner),
        in_specs=[VMEM] * 5,
        out_specs=[VMEM] * len(shapes),
        out_shape=shapes,
        compiler_params=params(),
        cost_estimate=cost(1_000_000_000, 3_000_000),
        name="inner_rows" if inner else "outer_rows",
    )(fields, along_lon, along_lat, displacement, edges)


def finish_kernel(groups, partial, weight, share, north, south, *refs):
    message, unit = refs[-2:]
    count = partial.shape[1]
    me = lax.axis_index("lev")
    unit[...] = jnp.full(unit.shape, 1.0 / SCALE, jnp.float32)
    for index, halo in enumerate((north, south)):
        wind, moved = weight[index], share[index]
        for field in range(count):
            advected = partial[index, field] + wind * halo[field]
            store_message(message, index, 2, field, count, advected, moved, groups, me)


def finish(partial, weight, share, north, south, after, groups):
    _, count, levels, _ = partial.shape
    f32 = jnp.float32
    return pl.pallas_call(
        functools.partial(finish_kernel, groups),
        in_specs=[VMEM] * (5 + len(after)),
        out_specs=[VMEM] * 2,
        out_shape=[
            jax.ShapeDtypeStruct((groups, message_height(2, count, levels), LANES), f32),
            jax.ShapeDtypeStruct((8, LANES), f32),
        ],
        compiler_params=params(),
        name="finish",
    )(partial, weight, share, north, south, *after)


def silu(value):
    half = 0.5 * value
    return half + half * jnp.tanh(half)


def layer(value, weight, bias, act):
    width = weight.shape[1]
    parts = []
    for start in range(0, width, 256):
        stop = min(start + 256, width)
        total = jnp.dot(value, weight[:, start:stop], preferred_element_type=jnp.float32)
        parts.append(act(total + bias[:, start:stop]).astype(jnp.bfloat16))
    return jnp.concatenate(parts, axis=1)


def active(own, lent, row):
    hits = jnp.logical_or(own[0] == row, lent[0] == row)
    return jnp.max(jnp.where(hits, 1.0, 0.0), axis=1, keepdims=True)


def physics_kernel(groups, helds, blocks, count, levels, aliased, *refs):
    sets = [refs[index * groups : (index + 1) * groups] for index in range(len(helds))]
    refs = refs[len(helds) * groups :]
    own, lent, first, bias_first, second, bias_second, third, bias_third = refs[:8]
    outs = refs[8 + aliased :]
    out, columns, carried, staged, sem = outs[0], *outs[-4:]
    if not aliased:
        outs[1][...] = jnp.full(outs[1].shape, 1.0 / SCALE, jnp.float32)
    me = lax.axis_index("lev")
    odd = lax.rem(lax.axis_index("lat"), 2)
    depth = groups * levels
    many = len(blocks)
    at = 0
    for parts, held in zip(sets, helds):
        tall = held * count * levels
        for step in range(groups):
            level = source(me, step, groups)
            part = parts[step]
            for index in range(held):
                for field in range(count):
                    start = pl.multiple_of(field * depth + level * levels, levels)
                    base = (index * count + field) * levels
                    columns[at + index, pl.ds(start, levels), :] = part[base : base + levels, :]
                low = tall + index * count
                carried[level, (at + index) * count : (at + index + 1) * count, :] = part[low : low + count, :]
        at += held
    for index in range(many):
        for field in range(count):
            for level in range(1, groups):
                row = field * depth + level * levels
                line = index * count + field
                columns[index, row : row + 1, :] += carried[level - 1, line : line + 1, :]
    value = jnp.concatenate([columns[index].astype(jnp.bfloat16) for index in range(many)], axis=1).T
    hidden = layer(value, first, bias_first, silu)
    hidden = layer(hidden, second, bias_second, silu)
    tendency = layer(hidden, third, bias_third, lambda v: v).T.astype(jnp.float32)

    def send(index, row):
        return pltpu.make_async_copy(staged.at[index], out.at[:, row, :], sem.at[index])

    for index, block in enumerate(blocks):
        part = tendency[:, index * LANES : (index + 1) * LANES]
        row = block[0] if block[0] == block[1] else jnp.where(odd == 1, block[1], block[0])
        staged[index] = columns[index] + jnp.where(active(own, lent, row) > 0.0, part, 0.0)
        if block[0] == block[1]:
            send(index, row).start()
            continue
        for parity in range(2):

            @pl.when(odd == parity)
            def _():
                send(index, block[parity]).start()

    for index, block in enumerate(blocks):
        send(index, block[0]).wait()


def physics(sets, network, rows, blocks, count, levels, result=None):
    groups = len(sets[0])
    many = len(blocks)
    width = count * groups * levels
    f32 = jnp.float32
    aliased = int(result is not None)
    unit = jax.ShapeDtypeStruct((8, LANES), f32)
    helds = [parts[0].shape[0] // (count * levels) for parts in sets]
    operands = [part for parts in sets for part in parts] + list(network)
    specs = [VMEM] * len(operands)
    if aliased:
        operands.append(result)
        specs.append(ANY)
    return pl.pallas_call(
        functools.partial(physics_kernel, groups, helds, blocks, count, levels, aliased),
        in_specs=specs,
        out_specs=[ANY] + [VMEM] * (1 - aliased),
        out_shape=[jax.ShapeDtypeStruct((width, rows, LANES), f32)] + [unit] * (1 - aliased),
        scratch_shapes=[
            pltpu.VMEM((many, width, LANES), f32),
            pltpu.VMEM((groups, -(-many * count // 8) * 8, LANES), f32),
            pltpu.VMEM((many, width, LANES), f32),
            pltpu.SemaphoreType.DMA((many,)),
        ],
        input_output_aliases={len(operands) - 1: 0} if aliased else {},
        compiler_params=params(),
        cost_estimate=cost(20_000_000_000, 5_000_000),
        name="physics",
    )(*operands)


def body(
    fields,
    courant_lon,
    courant_lat,
    displacement,
    own_slot,
    lent_slot,
    w_first,
    bias_first,
    w_second,
    bias_second,
    w_third,
    bias_third,
):
    count, levels, rows, lon = fields.shape
    groups = lax.axis_size("lev")
    bands = lax.axis_size("lat")
    even = lax.axis_index("lat") % 2 == 0
    half = jnp.float16
    f32 = jnp.float32

    near_pairs = [(i, i ^ 1) for i in range(bands) if i ^ 1 < bands]
    far_pairs = [(i, i + 1 if i % 2 else i - 1) for i in range(bands)]
    far_pairs = [(i, j) for i, j in far_pairs if 0 <= j < bands]
    edges = edge_rows(fields)
    far = lax.ppermute((jnp.where(even, edges[0], edges[1]) * SCALE).astype(half), "lat", far_pairs)
    near = lax.ppermute((jnp.where(even, edges[1], edges[0]) * SCALE).astype(half), "lat", near_pairs)

    def swap(message):
        sent = [(message[step] * SCALE).astype(half) for step in range(1, groups)]
        return [exchange(value, step + 1, groups) for step, value in enumerate(sent)]

    def received(message, values, unit):
        return [message[0]] + [value.astype(f32) * unit for value in values]

    local = (fields, courant_lon, courant_lat, displacement, edges, groups)
    network = (
        own_slot, lent_slot, w_first, bias_first.reshape(1, -1), w_second, bias_second.reshape(1, -1),
        w_third, bias_third.reshape(1, -1),
    )
    (inner,) = local_rows(True, *local)
    inner_moved = swap(inner)
    outer = local_rows(False, *local)
    north = jnp.where(even, far, near).astype(f32) * (1.0 / SCALE)
    south = jnp.where(even, near, far).astype(f32) * (1.0 / SCALE)
    message, unit = finish(*outer, north, south, (), groups)
    moved = swap(message)
    blocks = tuple((row, row) for row in range(1, rows - 1))
    sets = (received(inner, inner_moved, unit[0:1, :]),)
    result, unit = physics(sets, network, rows, blocks, count, levels)
    sets = (received(message, moved, unit[0:1, :]),)
    return physics(sets, network, rows, ((0, 0), (rows - 1, rows - 1)), count, levels, result)[0]


def solution(mesh):
    in_specs = (
        P(None, "lev", "lat", None),
        P("lev", "lat", None),
        P("lev", "lat", None),
        P("lev", "lat", None),
        P("lev", "lat", None),
        P("lev", "lat", None),
        P(),
        P(),
        P(),
        P(),
        P(),
        P(),
    )
    out_specs = P(None, "lat", "lev")
    return jax.shard_map(body, mesh=mesh, in_specs=in_specs, out_specs=out_specs, check_vma=False)
```

```python
import functools

import jax
import jax.numpy as jnp
from jax import lax
from jax.experimental import pallas as pl
from jax.experimental.pallas import tpu as pltpu
from jax.sharding import PartitionSpec as P

LANES = 128
SCALE = 4096.0
MEGA = 1024 * 1024
VMEM = pl.BlockSpec(memory_space=pltpu.VMEM)
ANY = pl.BlockSpec(memory_space=pl.ANY)


def place(me, other, count):
    if count & (count - 1) == 0:
        return lax.bitwise_xor(me, other)
    return lax.rem(other - me + count, count)


def source(me, step, count):
    if count & (count - 1) == 0:
        return lax.bitwise_xor(me, step)
    return lax.rem(me - step + count, count)


def exchange(value, step, count):
    power = count & (count - 1) == 0
    return lax.ppermute(value, "lev", [(i, i ^ step if power else (i + step) % count) for i in range(count)])


def params(mega=16):
    return pltpu.CompilerParams(vmem_limit_bytes=mega * MEGA)


def cost(flops, moved):
    return pl.CostEstimate(flops=flops, bytes_accessed=moved, transcendentals=0)


def edge_kernel(fields, out):
    out[0] = fields[:, :, 0, :]
    out[1] = fields[:, :, fields.shape[2] - 1, :]


def edge_rows(fields):
    count, levels, _, lon = fields.shape
    return pl.pallas_call(
        edge_kernel,
        in_specs=[VMEM],
        out_specs=VMEM,
        out_shape=jax.ShapeDtypeStruct((2, count, levels, lon), fields.dtype),
        compiler_params=params(),
        name="edge_rows",
    )(fields)


def message_height(rows, count, levels):
    return rows * count * levels + -(-rows * count // 8) * 8


def store_message(message, index, rows, field, count, advected, share, groups, me):
    levels = advected.shape[0]
    flux = share * advected
    depth = lax.broadcasted_iota(jnp.int32, flux.shape, 0)
    above = jnp.where(depth == 0, 0.0, pltpu.roll(flux, 1, 0))
    remapped = advected - flux + above
    base = (index * count + field) * levels
    row = rows * count * levels + index * count + field
    for group in range(groups):
        where = place(me, group, groups)
        lanes = slice(group * LANES, (group + 1) * LANES)
        message[where, base : base + levels, :] = remapped[:, lanes]
        message[where, row : row + 1, :] = flux[levels - 1 :, lanes]


def moved_share(displacement, row, me, groups):
    share = displacement[:, row, :]
    depth = lax.broadcasted_iota(jnp.int32, share.shape, 0)
    bottom = jnp.logical_and(depth == share.shape[0] - 1, me == groups - 1)
    return jnp.where(bottom, 0.0, share)


def winds(courant):
    return jnp.maximum(courant, 0.0), jnp.minimum(courant, 0.0)


def along_row(here, east_wind, west_wind):
    lon = here.shape[-1]
    result = here - east_wind * (here - pltpu.roll(here, 1, 1))
    return result - west_wind * (pltpu.roll(here, lon - 1, 1) - here)


def local_kernel(groups, inner, fields, along_lon, along_lat, displacement, edges, *outs):
    count, _, rows, _ = fields.shape
    me = lax.axis_index("lev")

    def line(row, field):
        return edges[int(row > 0), field] if row in (0, rows - 1) else fields[field, :, row, :]

    for row in range(1, rows - 1) if inner else (0, rows - 1):
        east_wind, west_wind = winds(along_lon[:, row, :])
        south_wind, north_wind = winds(along_lat[:, row, :])
        moved = moved_share(displacement, row, me, groups)
        index = int(row > 0)
        if not inner:
            outs[1][index] = -north_wind if row else south_wind
            outs[2][index] = moved
        for field in range(count):
            here = line(row, field)
            north = line(row - 1, field) if row else 0.0
            south = line(row + 1, field) if row < rows - 1 else 0.0
            result = along_row(here, east_wind, west_wind)
            result = result - south_wind * (here - north)
            result = result - north_wind * (south - here)
            if inner:
                store_message(outs[0], row - 1, rows - 2, field, count, result, moved, groups, me)
            else:
                outs[0][index, field] = result


def local_rows(inner, fields, along_lon, along_lat, displacement, edges, groups):
    count, levels, rows, lon = fields.shape
    f32 = jnp.float32
    shapes = [
        jax.ShapeDtypeStruct((2, count, levels, lon), f32),
        jax.ShapeDtypeStruct((2, levels, lon), f32),
        jax.ShapeDtypeStruct((2, levels, lon), f32),
    ]
    if inner:
        shapes = [jax.ShapeDtypeStruct((groups, message_height(rows - 2, count, levels), LANES), f32)]
    return pl.pallas_call(
        functools.partial(local_kernel, groups, inner),
        in_specs=[VMEM] * 5,
        out_specs=[VMEM] * len(shapes),
        out_shape=shapes,
        compiler_params=params(),
        cost_estimate=cost(1_000_000_000, 3_000_000),
        name="inner_rows" if inner else "outer_rows",
    )(fields, along_lon, along_lat, displacement, edges)


def finish_kernel(groups, partial, weight, share, north, south, *refs):
    message, unit = refs[-2:]
    count = partial.shape[1]
    me = lax.axis_index("lev")
    unit[...] = jnp.full(unit.shape, 1.0 / SCALE, jnp.float32)
    for index, halo in enumerate((north, south)):
        wind, moved = weight[index], share[index]
        for field in range(count):
            advected = partial[index, field] + wind * halo[field]
            store_message(message, index, 2, field, count, advected, moved, groups, me)


def finish(partial, weight, share, north, south, after, groups):
    _, count, levels, _ = partial.shape
    f32 = jnp.float32
    return pl.pallas_call(
        functools.partial(finish_kernel, groups),
        in_specs=[VMEM] * (5 + len(after)),
        out_specs=[VMEM] * 2,
        out_shape=[
            jax.ShapeDtypeStruct((groups, message_height(2, count, levels), LANES), f32),
            jax.ShapeDtypeStruct((8, LANES), f32),
        ],
        compiler_params=params(),
        name="finish",
    )(partial, weight, share, north, south, *after)


def silu(value):
    half = 0.5 * value
    return half + half * jnp.tanh(half)


def layer(value, weight, bias, act):
    width = weight.shape[1]
    parts = []
    for start in range(0, width, 256):
        stop = min(start + 256, width)
        total = jnp.dot(value, weight[:, start:stop], preferred_element_type=jnp.float32)
        parts.append(act(total + bias[:, start:stop]).astype(jnp.bfloat16))
    return jnp.concatenate(parts, axis=1)


def active(own, lent, row):
    hits = jnp.logical_or(own[0] == row, lent[0] == row)
    return jnp.max(jnp.where(hits, 1.0, 0.0), axis=1, keepdims=True)


def physics_kernel(groups, order, helds, blocks, count, levels, aliased, *refs):
    sets = [refs[index * groups : (index + 1) * groups] for index in range(len(helds))]
    refs = refs[len(helds) * groups :]
    own, lent, first, bias_first, second, bias_second, third, bias_third = refs[:8]
    outs = refs[8 + aliased :]
    out, columns, carried, staged, sem = outs[0], *outs[-4:]
    if not aliased:
        outs[1][...] = jnp.full(outs[1].shape, 1.0 / SCALE, jnp.float32)
    me = lax.axis_index("lev")
    odd = lax.rem(lax.axis_index("lat"), 2)
    depth = groups * levels
    many = len(blocks)
    at = 0
    for parts, held in zip(sets, helds):
        tall = held * count * levels
        for step, part in zip(order, parts):
            level = source(me, step, groups)
            for index in range(held):
                for field in range(count):
                    start = pl.multiple_of(field * depth + level * levels, levels)
                    base = (index * count + field) * levels
                    columns[at + index, pl.ds(start, levels), :] = part[base : base + levels, :]
                low = tall + index * count
                carried[level, (at + index) * count : (at + index + 1) * count, :] = part[low : low + count, :]
        at += held
    for index in range(many):
        for field in range(count):
            for level in range(1, groups):
                row = field * depth + level * levels
                line = index * count + field
                columns[index, row : row + 1, :] += carried[level - 1, line : line + 1, :]
    value = jnp.concatenate([columns[index].astype(jnp.bfloat16) for index in range(many)], axis=1).T
    hidden = layer(value, first, bias_first, silu)
    hidden = layer(hidden, second, bias_second, silu)
    tendency = layer(hidden, third, bias_third, lambda v: v).T.astype(jnp.float32)

    def send(index, row):
        return pltpu.make_async_copy(staged.at[index], out.at[:, row, :], sem.at[index])

    for index, block in enumerate(blocks):
        part = tendency[:, index * LANES : (index + 1) * LANES]
        row = block[0] if block[0] == block[1] else jnp.where(odd == 1, block[1], block[0])
        staged[index] = columns[index] + jnp.where(active(own, lent, row) > 0.0, part, 0.0)
        if block[0] == block[1]:
            send(index, row).start()
            continue
        for parity in range(2):

            @pl.when(odd == parity)
            def _():
                send(index, block[parity]).start()

    for index, block in enumerate(blocks):
        send(index, block[0]).wait()


def physics(sets, order, network, rows, blocks, count, levels, result=None):
    groups = len(sets[0])
    many = len(blocks)
    width = count * groups * levels
    f32 = jnp.float32
    aliased = int(result is not None)
    unit = jax.ShapeDtypeStruct((8, LANES), f32)
    helds = [parts[0].shape[0] // (count * levels) for parts in sets]
    operands = [part for parts in sets for part in parts] + list(network)
    specs = [VMEM] * len(operands)
    if aliased:
        operands.append(result)
        specs.append(ANY)
    return pl.pallas_call(
        functools.partial(physics_kernel, groups, order, helds, blocks, count, levels, aliased),
        in_specs=specs,
        out_specs=[ANY] + [VMEM] * (1 - aliased),
        out_shape=[jax.ShapeDtypeStruct((width, rows, LANES), f32)] + [unit] * (1 - aliased),
        scratch_shapes=[
            pltpu.VMEM((many, width, LANES), f32),
            pltpu.VMEM((groups, -(-many * count // 8) * 8, LANES), f32),
            pltpu.VMEM((many, width, LANES), f32),
            pltpu.SemaphoreType.DMA((many,)),
        ],
        input_output_aliases={len(operands) - 1: 0} if aliased else {},
        compiler_params=params(),
        cost_estimate=cost(20_000_000_000, 5_000_000),
        name="physics",
    )(*operands)


def body(
    fields,
    courant_lon,
    courant_lat,
    displacement,
    own_slot,
    lent_slot,
    w_first,
    bias_first,
    w_second,
    bias_second,
    w_third,
    bias_third,
):
    count, levels, rows, lon = fields.shape
    groups = lax.axis_size("lev")
    bands = lax.axis_size("lat")
    even = lax.axis_index("lat") % 2 == 0
    half = jnp.float16
    f32 = jnp.float32

    near_pairs = [(i, i ^ 1) for i in range(bands) if i ^ 1 < bands]
    far_pairs = [(i, i + 1 if i % 2 else i - 1) for i in range(bands)]
    far_pairs = [(i, j) for i, j in far_pairs if 0 <= j < bands]
    edges = edge_rows(fields)
    far = lax.ppermute((jnp.where(even, edges[0], edges[1]) * SCALE).astype(half), "lat", far_pairs)
    near = lax.ppermute((jnp.where(even, edges[1], edges[0]) * SCALE).astype(half), "lat", near_pairs)

    def swap(message):
        sent = [(message[step] * SCALE).astype(half) for step in range(1, groups)]
        return [exchange(value, step + 1, groups) for step, value in enumerate(sent)]

    def received(message, values, unit):
        taken = [message[0]] + [value.astype(f32) * unit for value in values]
        return [taken[step] for step in order]

    local = (fields, courant_lon, courant_lat, displacement, edges, groups)
    network = (
        own_slot, lent_slot, w_first, bias_first.reshape(1, -1), w_second, bias_second.reshape(1, -1),
        w_third, bias_third.reshape(1, -1),
    )
    (inner,) = local_rows(True, *local)
    inner_moved = swap(inner)
    outer = local_rows(False, *local)
    north = jnp.where(even, far, near).astype(f32) * (1.0 / SCALE)
    south = jnp.where(even, near, far).astype(f32) * (1.0 / SCALE)
    message, unit = finish(*outer, north, south, (), groups)
    moved = swap(message)
    blocks = tuple((row, row) for row in range(1, rows - 1))
    order = [0, *range(1, min(groups, 2)), *range(groups - 1, 1, -1)]
    sets = (received(inner, inner_moved, unit[0:1, :]),)
    result, unit = physics(sets, order, network, rows, blocks, count, levels)
    sets = (received(message, moved, unit[0:1, :]),)
    return physics(sets, order, network, rows, ((0, 0), (rows - 1, rows - 1)), count, levels, result)[0]


def solution(mesh):
    in_specs = (
        P(None, "lev", "lat", None),
        P("lev", "lat", None),
        P("lev", "lat", None),
        P("lev", "lat", None),
        P("lev", "lat", None),
        P("lev", "lat", None),
        P(),
        P(),
        P(),
        P(),
        P(),
        P(),
    )
    out_specs = P(None, "lat", "lev")
    return jax.shard_map(body, mesh=mesh, in_specs=in_specs, out_specs=out_specs, check_vma=False)
```

```python
import functools

import jax
import jax.numpy as jnp
from jax import lax
from jax.experimental import pallas as pl
from jax.experimental.pallas import tpu as pltpu
from jax.sharding import PartitionSpec as P

LANES = 128
SCALE = 4096.0
SETTLE = 0.87
MEGA = 1024 * 1024
VMEM = pl.BlockSpec(memory_space=pltpu.VMEM)
ANY = pl.BlockSpec(memory_space=pl.ANY)


def place(me, other, count):
    if count & (count - 1) == 0:
        return lax.bitwise_xor(me, other)
    return lax.rem(other - me + count, count)


def source(me, step, count):
    if count & (count - 1) == 0:
        return lax.bitwise_xor(me, step)
    return lax.rem(me - step + count, count)


def exchange(value, step, count):
    power = count & (count - 1) == 0
    return lax.ppermute(value, "lev", [(i, i ^ step if power else (i + step) % count) for i in range(count)])


def params(mega=16):
    return pltpu.CompilerParams(vmem_limit_bytes=mega * MEGA)


def cost(flops, moved):
    return pl.CostEstimate(flops=flops, bytes_accessed=moved, transcendentals=0)


def edge_kernel(fields, out):
    out[0] = fields[:, :, 0, :]
    out[1] = fields[:, :, fields.shape[2] - 1, :]


def edge_rows(fields):
    count, levels, _, lon = fields.shape
    return pl.pallas_call(
        edge_kernel,
        in_specs=[VMEM],
        out_specs=VMEM,
        out_shape=jax.ShapeDtypeStruct((2, count, levels, lon), fields.dtype),
        compiler_params=params(),
        name="edge_rows",
    )(fields)


def message_height(rows, count, levels):
    return rows * count * levels + -(-rows * count // 8) * 8


def settled(value):
    near = value.astype(jnp.bfloat16).astype(jnp.float32)
    return near + SETTLE * (value - near)


def store_message(message, index, rows, field, count, advected, share, groups, me):
    levels = advected.shape[0]
    flux = share * advected
    depth = lax.broadcasted_iota(jnp.int32, flux.shape, 0)
    above = jnp.where(depth == 0, 0.0, pltpu.roll(flux, 1, 0))
    remapped = settled(advected - flux + above)
    base = (index * count + field) * levels
    row = rows * count * levels + index * count + field
    for group in range(groups):
        where = place(me, group, groups)
        lanes = slice(group * LANES, (group + 1) * LANES)
        message[where, base : base + levels, :] = remapped[:, lanes]
        message[where, row : row + 1, :] = flux[levels - 1 :, lanes]


def moved_share(displacement, row, me, groups):
    share = displacement[:, row, :]
    depth = lax.broadcasted_iota(jnp.int32, share.shape, 0)
    bottom = jnp.logical_and(depth == share.shape[0] - 1, me == groups - 1)
    return jnp.where(bottom, 0.0, share)


def winds(courant):
    return jnp.maximum(courant, 0.0), jnp.minimum(courant, 0.0)


def along_row(here, east_wind, west_wind):
    lon = here.shape[-1]
    result = here - east_wind * (here - pltpu.roll(here, 1, 1))
    return result - west_wind * (pltpu.roll(here, lon - 1, 1) - here)


def local_kernel(groups, inner, fields, along_lon, along_lat, displacement, edges, *outs):
    count, _, rows, _ = fields.shape
    me = lax.axis_index("lev")

    def line(row, field):
        return edges[int(row > 0), field] if row in (0, rows - 1) else fields[field, :, row, :]

    for row in range(1, rows - 1) if inner else (0, rows - 1):
        east_wind, west_wind = winds(along_lon[:, row, :])
        south_wind, north_wind = winds(along_lat[:, row, :])
        moved = moved_share(displacement, row, me, groups)
        index = int(row > 0)
        if not inner:
            outs[1][index] = -north_wind if row else south_wind
            outs[2][index] = moved
        for field in range(count):
            here = line(row, field)
            north = line(row - 1, field) if row else 0.0
            south = line(row + 1, field) if row < rows - 1 else 0.0
            result = along_row(here, east_wind, west_wind)
            result = result - south_wind * (here - north)
            result = result - north_wind * (south - here)
            if inner:
                store_message(outs[0], row - 1, rows - 2, field, count, result, moved, groups, me)
            else:
                outs[0][index, field] = result


def local_rows(inner, fields, along_lon, along_lat, displacement, edges, groups):
    count, levels, rows, lon = fields.shape
    f32 = jnp.float32
    shapes = [
        jax.ShapeDtypeStruct((2, count, levels, lon), f32),
        jax.ShapeDtypeStruct((2, levels, lon), f32),
        jax.ShapeDtypeStruct((2, levels, lon), f32),
    ]
    if inner:
        shapes = [jax.ShapeDtypeStruct((groups, message_height(rows - 2, count, levels), LANES), f32)]
    return pl.pallas_call(
        functools.partial(local_kernel, groups, inner),
        in_specs=[VMEM] * 5,
        out_specs=[VMEM] * len(shapes),
        out_shape=shapes,
        compiler_params=params(),
        cost_estimate=cost(1_000_000_000, 3_000_000),
        name="inner_rows" if inner else "outer_rows",
    )(fields, along_lon, along_lat, displacement, edges)


def finish_kernel(groups, partial, weight, share, north, south, *refs):
    message, unit = refs[-2:]
    count = partial.shape[1]
    me = lax.axis_index("lev")
    unit[...] = jnp.full(unit.shape, 1.0 / SCALE, jnp.float32)
    for index, halo in enumerate((north, south)):
        wind, moved = weight[index], share[index]
        for field in range(count):
            advected = partial[index, field] + wind * halo[field]
            store_message(message, index, 2, field, count, advected, moved, groups, me)


def finish(partial, weight, share, north, south, after, groups):
    _, count, levels, _ = partial.shape
    f32 = jnp.float32
    return pl.pallas_call(
        functools.partial(finish_kernel, groups),
        in_specs=[VMEM] * (5 + len(after)),
        out_specs=[VMEM] * 2,
        out_shape=[
            jax.ShapeDtypeStruct((groups, message_height(2, count, levels), LANES), f32),
            jax.ShapeDtypeStruct((8, LANES), f32),
        ],
        compiler_params=params(),
        name="finish",
    )(partial, weight, share, north, south, *after)


def silu(value):
    half = 0.5 * value
    return half + half * jnp.tanh(half)


def layer(value, weight, bias, act):
    width = weight.shape[1]
    parts = []
    for start in range(0, width, 256):
        stop = min(start + 256, width)
        total = jnp.dot(value, weight[:, start:stop], preferred_element_type=jnp.float32)
        parts.append(act(total + bias[:, start:stop]).astype(jnp.bfloat16))
    return jnp.concatenate(parts, axis=1)


def active(own, lent, row):
    hits = jnp.logical_or(own[0] == row, lent[0] == row)
    return jnp.max(jnp.where(hits, 1.0, 0.0), axis=1, keepdims=True)


def physics_kernel(groups, order, helds, blocks, count, levels, aliased, *refs):
    sets = [refs[index * groups : (index + 1) * groups] for index in range(len(helds))]
    refs = refs[len(helds) * groups :]
    own, lent, first, bias_first, second, bias_second, third, bias_third = refs[:8]
    outs = refs[8 + aliased :]
    out, columns, carried, staged, sem = outs[0], *outs[-4:]
    if not aliased:
        outs[1][...] = jnp.full(outs[1].shape, 1.0 / SCALE, jnp.float32)
    me = lax.axis_index("lev")
    odd = lax.rem(lax.axis_index("lat"), 2)
    depth = groups * levels
    many = len(blocks)
    at = 0
    for parts, held in zip(sets, helds):
        tall = held * count * levels
        for step, part in zip(order, parts):
            level = source(me, step, groups)
            for index in range(held):
                for field in range(count):
                    start = pl.multiple_of(field * depth + level * levels, levels)
                    base = (index * count + field) * levels
                    columns[at + index, pl.ds(start, levels), :] = part[base : base + levels, :]
                low = tall + index * count
                carried[level, (at + index) * count : (at + index + 1) * count, :] = part[low : low + count, :]
        at += held
    for index in range(many):
        for field in range(count):
            for level in range(1, groups):
                row = field * depth + level * levels
                line = index * count + field
                columns[index, row : row + 1, :] += carried[level - 1, line : line + 1, :]
    value = jnp.concatenate([columns[index].astype(jnp.bfloat16) for index in range(many)], axis=1).T
    hidden = layer(value, first, bias_first, silu)
    hidden = layer(hidden, second, bias_second, silu)
    tendency = layer(hidden, third, bias_third, lambda v: v).T.astype(jnp.float32)

    def send(index, row):
        return pltpu.make_async_copy(staged.at[index], out.at[:, row, :], sem.at[index])

    for index, block in enumerate(blocks):
        part = tendency[:, index * LANES : (index + 1) * LANES]
        row = block[0] if block[0] == block[1] else jnp.where(odd == 1, block[1], block[0])
        staged[index] = columns[index] + jnp.where(active(own, lent, row) > 0.0, part, 0.0)
        if block[0] == block[1]:
            send(index, row).start()
            continue
        for parity in range(2):

            @pl.when(odd == parity)
            def _():
                send(index, block[parity]).start()

    for index, block in enumerate(blocks):
        send(index, block[0]).wait()


def physics(sets, order, network, rows, blocks, count, levels, result=None):
    groups = len(sets[0])
    many = len(blocks)
    width = count * groups * levels
    f32 = jnp.float32
    aliased = int(result is not None)
    unit = jax.ShapeDtypeStruct((8, LANES), f32)
    helds = [parts[0].shape[0] // (count * levels) for parts in sets]
    operands = [part for parts in sets for part in parts] + list(network)
    specs = [VMEM] * len(operands)
    if aliased:
        operands.append(result)
        specs.append(ANY)
    return pl.pallas_call(
        functools.partial(physics_kernel, groups, order, helds, blocks, count, levels, aliased),
        in_specs=specs,
        out_specs=[ANY] + [VMEM] * (1 - aliased),
        out_shape=[jax.ShapeDtypeStruct((width, rows, LANES), f32)] + [unit] * (1 - aliased),
        scratch_shapes=[
            pltpu.VMEM((many, width, LANES), f32),
            pltpu.VMEM((groups, -(-many * count // 8) * 8, LANES), f32),
            pltpu.VMEM((many, width, LANES), f32),
            pltpu.SemaphoreType.DMA((many,)),
        ],
        input_output_aliases={len(operands) - 1: 0} if aliased else {},
        compiler_params=params(),
        cost_estimate=cost(20_000_000_000, 5_000_000),
        name="physics",
    )(*operands)


def body(
    fields,
    courant_lon,
    courant_lat,
    displacement,
    own_slot,
    lent_slot,
    w_first,
    bias_first,
    w_second,
    bias_second,
    w_third,
    bias_third,
):
    count, levels, rows, lon = fields.shape
    groups = lax.axis_size("lev")
    bands = lax.axis_size("lat")
    even = lax.axis_index("lat") % 2 == 0
    half = jnp.float16
    f32 = jnp.float32

    near_pairs = [(i, i ^ 1) for i in range(bands) if i ^ 1 < bands]
    far_pairs = [(i, i + 1 if i % 2 else i - 1) for i in range(bands)]
    far_pairs = [(i, j) for i, j in far_pairs if 0 <= j < bands]
    edges = edge_rows(fields)
    far = lax.ppermute((jnp.where(even, edges[0], edges[1]) * SCALE).astype(half), "lat", far_pairs)
    near = lax.ppermute((jnp.where(even, edges[1], edges[0]) * SCALE).astype(half), "lat", near_pairs)

    def swap(message):
        sent = [(message[step] * SCALE).astype(half) for step in range(1, groups)]
        return [exchange(value, step + 1, groups) for step, value in enumerate(sent)]

    def received(message, values, unit):
        taken = [message[0]] + [value.astype(f32) * unit for value in values]
        return [taken[step] for step in order]

    local = (fields, courant_lon, courant_lat, displacement, edges, groups)
    network = (
        own_slot, lent_slot, w_first, bias_first.reshape(1, -1), w_second, bias_second.reshape(1, -1),
        w_third, bias_third.reshape(1, -1),
    )
    (inner,) = local_rows(True, *local)
    inner_moved = swap(inner)
    outer = local_rows(False, *local)
    north = jnp.where(even, far, near).astype(f32) * (1.0 / SCALE)
    south = jnp.where(even, near, far).astype(f32) * (1.0 / SCALE)
    message, unit = finish(*outer, north, south, (), groups)
    moved = swap(message)
    blocks = tuple((row, row) for row in range(1, rows - 1))
    order = [0, *range(1, min(groups, 2)), *range(groups - 1, 1, -1)]
    sets = (received(inner, inner_moved, unit[0:1, :]),)
    result, unit = physics(sets, order, network, rows, blocks, count, levels)
    sets = (received(message, moved, unit[0:1, :]),)
    return physics(sets, order, network, rows, ((0, 0), (rows - 1, rows - 1)), count, levels, result)[0]


def solution(mesh):
    in_specs = (
        P(None, "lev", "lat", None),
        P("lev", "lat", None),
        P("lev", "lat", None),
        P("lev", "lat", None),
        P("lev", "lat", None),
        P("lev", "lat", None),
        P(),
        P(),
        P(),
        P(),
        P(),
        P(),
    )
    out_specs = P(None, "lat", "lev")
    return jax.shard_map(body, mesh=mesh, in_specs=in_specs, out_specs=out_specs, check_vma=False)
```

```python
import functools

import jax
import jax.numpy as jnp
from jax import lax
from jax.experimental import pallas as pl
from jax.experimental.pallas import tpu as pltpu
from jax.sharding import PartitionSpec as P

LANES = 128
SCALE = 4096.0
SETTLE = 0.87
MEGA = 1024 * 1024
VMEM = pl.BlockSpec(memory_space=pltpu.VMEM)
ANY = pl.BlockSpec(memory_space=pl.ANY)


def place(me, other, count):
    if count & (count - 1) == 0:
        return lax.bitwise_xor(me, other)
    return lax.rem(other - me + count, count)


def source(me, step, count):
    if count & (count - 1) == 0:
        return lax.bitwise_xor(me, step)
    return lax.rem(me - step + count, count)


def exchange(value, step, count):
    power = count & (count - 1) == 0
    return lax.ppermute(value, "lev", [(i, i ^ step if power else (i + step) % count) for i in range(count)])


def params(mega=16):
    return pltpu.CompilerParams(vmem_limit_bytes=mega * MEGA)


def cost(flops, moved):
    return pl.CostEstimate(flops=flops, bytes_accessed=moved, transcendentals=0)


def edge_kernel(fields, out):
    out[0] = fields[:, :, 0, :]
    out[1] = fields[:, :, fields.shape[2] - 1, :]


def edge_rows(fields):
    count, levels, _, lon = fields.shape
    return pl.pallas_call(
        edge_kernel,
        in_specs=[VMEM],
        out_specs=VMEM,
        out_shape=jax.ShapeDtypeStruct((2, count, levels, lon), fields.dtype),
        compiler_params=params(),
        name="edge_rows",
    )(fields)


def message_height(rows, count, levels):
    return rows * count * levels + -(-rows * count // 8) * 8


def settled(value):
    near = value.astype(jnp.bfloat16).astype(jnp.float32)
    return near + SETTLE * (value - near)


def store_message(message, index, rows, field, count, advected, share, groups, me):
    levels = advected.shape[0]
    flux = share * advected
    depth = lax.broadcasted_iota(jnp.int32, flux.shape, 0)
    above = jnp.where(depth == 0, 0.0, pltpu.roll(flux, 1, 0))
    remapped = settled(advected - flux + above)
    base = (index * count + field) * levels
    row = rows * count * levels + index * count + field
    for group in range(groups):
        where = place(me, group, groups)
        lanes = slice(group * LANES, (group + 1) * LANES)
        message[where, base : base + levels, :] = remapped[:, lanes]
        message[where, row : row + 1, :] = flux[levels - 1 :, lanes]


def moved_share(displacement, row, me, groups):
    share = displacement[:, row, :]
    depth = lax.broadcasted_iota(jnp.int32, share.shape, 0)
    bottom = jnp.logical_and(depth == share.shape[0] - 1, me == groups - 1)
    return jnp.where(bottom, 0.0, share)


def winds(courant):
    return jnp.maximum(courant, 0.0), jnp.minimum(courant, 0.0)


def along_row(here, east_wind, west_wind):
    lon = here.shape[-1]
    result = here - east_wind * (here - pltpu.roll(here, 1, 1))
    return result - west_wind * (pltpu.roll(here, lon - 1, 1) - here)


def local_kernel(groups, inner, fields, along_lon, along_lat, displacement, edges, *outs):
    count, _, rows, _ = fields.shape
    me = lax.axis_index("lev")

    def line(row, field):
        return edges[int(row > 0), field] if row in (0, rows - 1) else fields[field, :, row, :]

    for row in range(1, rows - 1) if inner else (0, rows - 1):
        east_wind, west_wind = winds(along_lon[:, row, :])
        south_wind, north_wind = winds(along_lat[:, row, :])
        moved = moved_share(displacement, row, me, groups)
        index = int(row > 0)
        if not inner:
            outs[1][index] = -north_wind if row else south_wind
            outs[2][index] = moved
        for field in range(count):
            here = line(row, field)
            north = line(row - 1, field) if row else 0.0
            south = line(row + 1, field) if row < rows - 1 else 0.0
            result = along_row(here, east_wind, west_wind)
            result = result - south_wind * (here - north)
            result = result - north_wind * (south - here)
            if inner:
                store_message(outs[0], row - 1, rows - 2, field, count, result, moved, groups, me)
            else:
                outs[0][index, field] = result


def local_rows(inner, fields, along_lon, along_lat, displacement, edges, groups):
    count, levels, rows, lon = fields.shape
    f32 = jnp.float32
    shapes = [
        jax.ShapeDtypeStruct((2, count, levels, lon), f32),
        jax.ShapeDtypeStruct((2, levels, lon), f32),
        jax.ShapeDtypeStruct((2, levels, lon), f32),
    ]
    if inner:
        shapes = [jax.ShapeDtypeStruct((groups, message_height(rows - 2, count, levels), LANES), f32)]
    return pl.pallas_call(
        functools.partial(local_kernel, groups, inner),
        in_specs=[VMEM] * 5,
        out_specs=[VMEM] * len(shapes),
        out_shape=shapes,
        compiler_params=params(),
        cost_estimate=cost(1_000_000_000, 3_000_000),
        name="inner_rows" if inner else "outer_rows",
    )(fields, along_lon, along_lat, displacement, edges)


def finish_row(groups, far, rows, partial, weight, share, halo, message):
    count = partial.shape[1]
    me = lax.axis_index("lev")
    odd = lax.rem(lax.axis_index("lat"), 2)
    index = odd if far else 1 - odd
    wind, moved = weight[index], share[index]
    for field in range(count):
        advected = partial[index, field] + wind * halo[field]
        store_message(message, int(far), rows, field, count, advected, moved, groups, me)


def near_kernel(groups, partial, weight, share, halo, message):
    finish_row(groups, False, 1, partial, weight, share, halo, message)


def far_kernel(groups, partial, weight, share, halo, near, message, unit):
    count, levels = partial.shape[1:3]
    size = count * levels
    unit[...] = jnp.full(unit.shape, 1.0 / SCALE, jnp.float32)
    message[:, 0:size, :] = near[:, 0:size, :]
    message[:, 2 * size : 2 * size + count, :] = near[:, size : size + count, :]
    finish_row(groups, True, 2, partial, weight, share, halo, message)


def near_finish(partial, weight, share, halo, groups):
    _, count, levels, _ = partial.shape
    return pl.pallas_call(
        functools.partial(near_kernel, groups),
        in_specs=[VMEM] * 4,
        out_specs=VMEM,
        out_shape=jax.ShapeDtypeStruct((groups, message_height(1, count, levels), LANES), jnp.float32),
        compiler_params=params(),
        name="near_finish",
    )(partial, weight, share, halo)


def far_finish(partial, weight, share, halo, near, groups):
    _, count, levels, _ = partial.shape
    f32 = jnp.float32
    return pl.pallas_call(
        functools.partial(far_kernel, groups),
        in_specs=[VMEM] * 5,
        out_specs=[VMEM] * 2,
        out_shape=[
            jax.ShapeDtypeStruct((groups, message_height(2, count, levels), LANES), f32),
            jax.ShapeDtypeStruct((8, LANES), f32),
        ],
        compiler_params=params(),
        name="far_finish",
    )(partial, weight, share, halo, near)


def silu(value):
    half = 0.5 * value
    return half + half * jnp.tanh(half)


def layer(value, weight, bias, act):
    width = weight.shape[1]
    parts = []
    for start in range(0, width, 256):
        stop = min(start + 256, width)
        total = jnp.dot(value, weight[:, start:stop], preferred_element_type=jnp.float32)
        parts.append(act(total + bias[:, start:stop]).astype(jnp.bfloat16))
    return jnp.concatenate(parts, axis=1)


def active(own, lent, row):
    hits = jnp.logical_or(own[0] == row, lent[0] == row)
    return jnp.max(jnp.where(hits, 1.0, 0.0), axis=1, keepdims=True)


def physics_kernel(groups, order, helds, blocks, count, levels, aliased, *refs):
    sets = [refs[index * groups : (index + 1) * groups] for index in range(len(helds))]
    refs = refs[len(helds) * groups :]
    own, lent, first, bias_first, second, bias_second, third, bias_third = refs[:8]
    outs = refs[8 + aliased :]
    out, columns, carried, staged, sem = outs[0], *outs[-4:]
    if not aliased:
        outs[1][...] = jnp.full(outs[1].shape, 1.0 / SCALE, jnp.float32)
    me = lax.axis_index("lev")
    odd = lax.rem(lax.axis_index("lat"), 2)
    depth = groups * levels
    many = len(blocks)
    at = 0
    for parts, held in zip(sets, helds):
        tall = held * count * levels
        for step, part in zip(order, parts):
            level = source(me, step, groups)
            for index in range(held):
                for field in range(count):
                    start = pl.multiple_of(field * depth + level * levels, levels)
                    base = (index * count + field) * levels
                    columns[at + index, pl.ds(start, levels), :] = part[base : base + levels, :]
                low = tall + index * count
                carried[level, (at + index) * count : (at + index + 1) * count, :] = part[low : low + count, :]
        at += held
    for index in range(many):
        for field in range(count):
            for level in range(1, groups):
                row = field * depth + level * levels
                line = index * count + field
                columns[index, row : row + 1, :] += carried[level - 1, line : line + 1, :]
    value = jnp.concatenate([columns[index].astype(jnp.bfloat16) for index in range(many)], axis=1).T
    hidden = layer(value, first, bias_first, silu)
    hidden = layer(hidden, second, bias_second, silu)
    tendency = layer(hidden, third, bias_third, lambda v: v).T.astype(jnp.float32)

    def send(index, row):
        return pltpu.make_async_copy(staged.at[index], out.at[:, row, :], sem.at[index])

    for index, block in enumerate(blocks):
        part = tendency[:, index * LANES : (index + 1) * LANES]
        row = block[0] if block[0] == block[1] else jnp.where(odd == 1, block[1], block[0])
        staged[index] = columns[index] + jnp.where(active(own, lent, row) > 0.0, part, 0.0)
        if block[0] == block[1]:
            send(index, row).start()
            continue
        for parity in range(2):

            @pl.when(odd == parity)
            def _():
                send(index, block[parity]).start()

    for index, block in enumerate(blocks):
        send(index, block[0]).wait()


def physics(sets, order, network, rows, blocks, count, levels, result=None):
    groups = len(sets[0])
    many = len(blocks)
    width = count * groups * levels
    f32 = jnp.float32
    aliased = int(result is not None)
    unit = jax.ShapeDtypeStruct((8, LANES), f32)
    helds = [parts[0].shape[0] // (count * levels) for parts in sets]
    operands = [part for parts in sets for part in parts] + list(network)
    specs = [VMEM] * len(operands)
    if aliased:
        operands.append(result)
        specs.append(ANY)
    return pl.pallas_call(
        functools.partial(physics_kernel, groups, order, helds, blocks, count, levels, aliased),
        in_specs=specs,
        out_specs=[ANY] + [VMEM] * (1 - aliased),
        out_shape=[jax.ShapeDtypeStruct((width, rows, LANES), f32)] + [unit] * (1 - aliased),
        scratch_shapes=[
            pltpu.VMEM((many, width, LANES), f32),
            pltpu.VMEM((groups, -(-many * count // 8) * 8, LANES), f32),
            pltpu.VMEM((many, width, LANES), f32),
            pltpu.SemaphoreType.DMA((many,)),
        ],
        input_output_aliases={len(operands) - 1: 0} if aliased else {},
        compiler_params=params(),
        cost_estimate=cost(20_000_000_000, 5_000_000),
        name="physics",
    )(*operands)


def body(
    fields,
    courant_lon,
    courant_lat,
    displacement,
    own_slot,
    lent_slot,
    w_first,
    bias_first,
    w_second,
    bias_second,
    w_third,
    bias_third,
):
    count, levels, rows, lon = fields.shape
    groups = lax.axis_size("lev")
    bands = lax.axis_size("lat")
    even = lax.axis_index("lat") % 2 == 0
    half = jnp.float16
    f32 = jnp.float32

    near_pairs = [(i, i ^ 1) for i in range(bands) if i ^ 1 < bands]
    far_pairs = [(i, i + 1 if i % 2 else i - 1) for i in range(bands)]
    far_pairs = [(i, j) for i, j in far_pairs if 0 <= j < bands]
    edges = edge_rows(fields)
    far = lax.ppermute((jnp.where(even, edges[0], edges[1]) * SCALE).astype(half), "lat", far_pairs)
    near = lax.ppermute((jnp.where(even, edges[1], edges[0]) * SCALE).astype(half), "lat", near_pairs)

    def swap(message):
        sent = [(message[step] * SCALE).astype(half) for step in range(1, groups)]
        return [exchange(value, step + 1, groups) for step, value in enumerate(sent)]

    def received(message, values, unit):
        taken = [message[0]] + [value.astype(f32) * unit for value in values]
        return [taken[step] for step in order]

    local = (fields, courant_lon, courant_lat, displacement, edges, groups)
    network = (
        own_slot, lent_slot, w_first, bias_first.reshape(1, -1), w_second, bias_second.reshape(1, -1),
        w_third, bias_third.reshape(1, -1),
    )
    (inner,) = local_rows(True, *local)
    inner_moved = swap(inner)
    outer = local_rows(False, *local)
    near_message = near_finish(*outer, near.astype(f32) * (1.0 / SCALE), groups)
    message, unit = far_finish(*outer, far.astype(f32) * (1.0 / SCALE), near_message, groups)
    moved = swap(message)
    blocks = tuple((row, row) for row in range(1, rows - 1))
    order = [0, *range(1, min(groups, 2)), *range(groups - 1, 1, -1)]
    sets = (received(inner, inner_moved, unit[0:1, :]),)
    result, unit = physics(sets, order, network, rows, blocks, count, levels)
    sets = (received(message, moved, unit[0:1, :]),)
    return physics(sets, order, network, rows, ((rows - 1, 0), (0, rows - 1)), count, levels, result)[0]


def solution(mesh):
    in_specs = (
        P(None, "lev", "lat", None),
        P("lev", "lat", None),
        P("lev", "lat", None),
        P("lev", "lat", None),
        P("lev", "lat", None),
        P("lev", "lat", None),
        P(),
        P(),
        P(),
        P(),
        P(),
        P(),
    )
    out_specs = P(None, "lat", "lev")
    return jax.shard_map(body, mesh=mesh, in_specs=in_specs, out_specs=out_specs, check_vma=False)
```

```python
import functools

import jax
import jax.numpy as jnp
from jax import lax
from jax.experimental import pallas as pl
from jax.experimental.pallas import tpu as pltpu
from jax.sharding import PartitionSpec as P

LANES = 128
SCALE = 4096.0
SETTLE = 0.87
MEGA = 1024 * 1024
VMEM = pl.BlockSpec(memory_space=pltpu.VMEM)
ANY = pl.BlockSpec(memory_space=pl.ANY)


def place(me, other, count):
    if count & (count - 1) == 0:
        return lax.bitwise_xor(me, other)
    return lax.rem(other - me + count, count)


def source(me, step, count):
    if count & (count - 1) == 0:
        return lax.bitwise_xor(me, step)
    return lax.rem(me - step + count, count)


def exchange(value, step, count):
    power = count & (count - 1) == 0
    return lax.ppermute(value, "lev", [(i, i ^ step if power else (i + step) % count) for i in range(count)])


def params(mega=16):
    return pltpu.CompilerParams(vmem_limit_bytes=mega * MEGA)


def cost(flops, moved):
    return pl.CostEstimate(flops=flops, bytes_accessed=moved, transcendentals=0)


def edge_kernel(fields, out):
    odd = lax.rem(lax.axis_index("lat"), 2)
    out[1 - odd] = fields[:, :, 0, :]
    out[odd] = fields[:, :, fields.shape[2] - 1, :]


def edge_rows(fields):
    count, levels, _, lon = fields.shape
    return pl.pallas_call(
        edge_kernel,
        in_specs=[VMEM],
        out_specs=VMEM,
        out_shape=jax.ShapeDtypeStruct((2, count, levels, lon), fields.dtype),
        compiler_params=params(),
        name="edge_rows",
    )(fields)


def message_height(rows, count, levels):
    return rows * count * levels + -(-rows * count // 8) * 8


def settled(value):
    near = value.astype(jnp.bfloat16).astype(jnp.float32)
    return near + SETTLE * (value - near)


def store_message(message, index, rows, field, count, advected, share, groups, me):
    levels = advected.shape[0]
    flux = share * advected
    depth = lax.broadcasted_iota(jnp.int32, flux.shape, 0)
    above = jnp.where(depth == 0, 0.0, pltpu.roll(flux, 1, 0))
    remapped = settled(advected - flux + above)
    base = (index * count + field) * levels
    row = rows * count * levels + index * count + field
    for group in range(groups):
        where = place(me, group, groups)
        lanes = slice(group * LANES, (group + 1) * LANES)
        message[where, base : base + levels, :] = remapped[:, lanes]
        message[where, row : row + 1, :] = flux[levels - 1 :, lanes]


def moved_share(displacement, row, me, groups):
    share = displacement[:, row, :]
    depth = lax.broadcasted_iota(jnp.int32, share.shape, 0)
    bottom = jnp.logical_and(depth == share.shape[0] - 1, me == groups - 1)
    return jnp.where(bottom, 0.0, share)


def winds(courant):
    return jnp.maximum(courant, 0.0), jnp.minimum(courant, 0.0)


def along_row(here, east_wind, west_wind):
    lon = here.shape[-1]
    result = here - east_wind * (here - pltpu.roll(here, 1, 1))
    return result - west_wind * (pltpu.roll(here, lon - 1, 1) - here)


def local_kernel(groups, inner, fields, along_lon, along_lat, displacement, edges, *outs):
    count, _, rows, _ = fields.shape
    me = lax.axis_index("lev")
    odd = lax.rem(lax.axis_index("lat"), 2)

    def line(row, field):
        return edges[odd if row else 1 - odd, field] if row in (0, rows - 1) else fields[field, :, row, :]

    for row in range(1, rows - 1) if inner else (0, rows - 1):
        east_wind, west_wind = winds(along_lon[:, row, :])
        south_wind, north_wind = winds(along_lat[:, row, :])
        moved = moved_share(displacement, row, me, groups)
        index = int(row > 0)
        if not inner:
            outs[1][index] = -north_wind if row else south_wind
            outs[2][index] = moved
        for field in range(count):
            here = line(row, field)
            north = line(row - 1, field) if row else 0.0
            south = line(row + 1, field) if row < rows - 1 else 0.0
            result = along_row(here, east_wind, west_wind)
            result = result - south_wind * (here - north)
            result = result - north_wind * (south - here)
            if inner:
                store_message(outs[0], row - 1, rows - 2, field, count, result, moved, groups, me)
            else:
                outs[0][index, field] = result


def local_rows(inner, fields, along_lon, along_lat, displacement, edges, groups):
    count, levels, rows, lon = fields.shape
    f32 = jnp.float32
    shapes = [
        jax.ShapeDtypeStruct((2, count, levels, lon), f32),
        jax.ShapeDtypeStruct((2, levels, lon), f32),
        jax.ShapeDtypeStruct((2, levels, lon), f32),
    ]
    if inner:
        shapes = [jax.ShapeDtypeStruct((groups, message_height(rows - 2, count, levels), LANES), f32)]
    return pl.pallas_call(
        functools.partial(local_kernel, groups, inner),
        in_specs=[VMEM] * 5,
        out_specs=[VMEM] * len(shapes),
        out_shape=shapes,
        compiler_params=params(),
        cost_estimate=cost(1_000_000_000, 3_000_000),
        name="inner_rows" if inner else "outer_rows",
    )(fields, along_lon, along_lat, displacement, edges)


def finish_row(groups, far, rows, partial, weight, share, halo, message):
    count = partial.shape[1]
    me = lax.axis_index("lev")
    odd = lax.rem(lax.axis_index("lat"), 2)
    index = odd if far else 1 - odd
    wind, moved = weight[index], share[index]
    for field in range(count):
        advected = partial[index, field] + wind * halo[field]
        store_message(message, int(far), rows, field, count, advected, moved, groups, me)


def near_kernel(groups, partial, weight, share, halo, message):
    finish_row(groups, False, 1, partial, weight, share, halo, message)


def far_kernel(groups, partial, weight, share, halo, near, message, unit):
    count, levels = partial.shape[1:3]
    size = count * levels
    unit[...] = jnp.full(unit.shape, 1.0 / SCALE, jnp.float32)
    message[:, 0:size, :] = near[:, 0:size, :]
    message[:, 2 * size : 2 * size + count, :] = near[:, size : size + count, :]
    finish_row(groups, True, 2, partial, weight, share, halo, message)


def near_finish(partial, weight, share, halo, groups):
    _, count, levels, _ = partial.shape
    return pl.pallas_call(
        functools.partial(near_kernel, groups),
        in_specs=[VMEM] * 4,
        out_specs=VMEM,
        out_shape=jax.ShapeDtypeStruct((groups, message_height(1, count, levels), LANES), jnp.float32),
        compiler_params=params(),
        name="near_finish",
    )(partial, weight, share, halo)


def far_finish(partial, weight, share, halo, near, groups):
    _, count, levels, _ = partial.shape
    f32 = jnp.float32
    return pl.pallas_call(
        functools.partial(far_kernel, groups),
        in_specs=[VMEM] * 5,
        out_specs=[VMEM] * 2,
        out_shape=[
            jax.ShapeDtypeStruct((groups, message_height(2, count, levels), LANES), f32),
            jax.ShapeDtypeStruct((8, LANES), f32),
        ],
        compiler_params=params(),
        name="far_finish",
    )(partial, weight, share, halo, near)


def silu(value):
    half = 0.5 * value
    return half + half * jnp.tanh(half)


def layer(value, weight, bias, act):
    width = weight.shape[1]
    parts = []
    for start in range(0, width, 256):
        stop = min(start + 256, width)
        total = jnp.dot(value, weight[:, start:stop], preferred_element_type=jnp.float32)
        parts.append(act(total + bias[:, start:stop]).astype(jnp.bfloat16))
    return jnp.concatenate(parts, axis=1)


def active(own, lent, row):
    hits = jnp.logical_or(own[0] == row, lent[0] == row)
    return jnp.max(jnp.where(hits, 1.0, 0.0), axis=1, keepdims=True)


def physics_kernel(groups, order, helds, blocks, count, levels, aliased, *refs):
    sets = [refs[index * groups : (index + 1) * groups] for index in range(len(helds))]
    refs = refs[len(helds) * groups :]
    own, lent, first, bias_first, second, bias_second, third, bias_third = refs[:8]
    outs = refs[8 + aliased :]
    out, columns, carried, staged, sem = outs[0], *outs[-4:]
    if not aliased:
        outs[1][...] = jnp.full(outs[1].shape, 1.0 / SCALE, jnp.float32)
    me = lax.axis_index("lev")
    odd = lax.rem(lax.axis_index("lat"), 2)
    depth = groups * levels
    many = len(blocks)
    at = 0
    for parts, held in zip(sets, helds):
        tall = held * count * levels
        for step, part in zip(order, parts):
            level = source(me, step, groups)
            for index in range(held):
                for field in range(count):
                    start = pl.multiple_of(field * depth + level * levels, levels)
                    base = (index * count + field) * levels
                    columns[at + index, pl.ds(start, levels), :] = part[base : base + levels, :]
                low = tall + index * count
                carried[level, (at + index) * count : (at + index + 1) * count, :] = part[low : low + count, :]
        at += held
    for index in range(many):
        for field in range(count):
            for level in range(1, groups):
                row = field * depth + level * levels
                line = index * count + field
                columns[index, row : row + 1, :] += carried[level - 1, line : line + 1, :]
    value = jnp.concatenate([columns[index].astype(jnp.bfloat16) for index in range(many)], axis=1).T
    hidden = layer(value, first, bias_first, silu)
    hidden = layer(hidden, second, bias_second, silu)
    tendency = layer(hidden, third, bias_third, lambda v: v)

    def send(index, row):
        return pltpu.make_async_copy(staged.at[index], out.at[:, row, :], sem.at[index])

    for index, block in enumerate(blocks):
        part = tendency[index * LANES : (index + 1) * LANES, :].T.astype(jnp.float32)
        row = block[0] if block[0] == block[1] else jnp.where(odd == 1, block[1], block[0])
        staged[index] = columns[index] + jnp.where(active(own, lent, row) > 0.0, part, 0.0)
        if block[0] == block[1]:
            send(index, row).start()
            continue
        for parity in range(2):

            @pl.when(odd == parity)
            def _():
                send(index, block[parity]).start()

    for index, block in enumerate(blocks):
        send(index, block[0]).wait()


def physics(sets, order, network, rows, blocks, count, levels, result=None):
    groups = len(sets[0])
    many = len(blocks)
    width = count * groups * levels
    f32 = jnp.float32
    aliased = int(result is not None)
    unit = jax.ShapeDtypeStruct((8, LANES), f32)
    helds = [parts[0].shape[0] // (count * levels) for parts in sets]
    operands = [part for parts in sets for part in parts] + list(network)
    specs = [VMEM] * len(operands)
    if aliased:
        operands.append(result)
        specs.append(ANY)
    return pl.pallas_call(
        functools.partial(physics_kernel, groups, order, helds, blocks, count, levels, aliased),
        in_specs=specs,
        out_specs=[ANY] + [VMEM] * (1 - aliased),
        out_shape=[jax.ShapeDtypeStruct((width, rows, LANES), f32)] + [unit] * (1 - aliased),
        scratch_shapes=[
            pltpu.VMEM((many, width, LANES), f32),
            pltpu.VMEM((groups, -(-many * count // 8) * 8, LANES), f32),
            pltpu.VMEM((many, width, LANES), f32),
            pltpu.SemaphoreType.DMA((many,)),
        ],
        input_output_aliases={len(operands) - 1: 0} if aliased else {},
        compiler_params=params(),
        cost_estimate=cost(20_000_000_000, 5_000_000),
        name="physics",
    )(*operands)


def body(
    fields,
    courant_lon,
    courant_lat,
    displacement,
    own_slot,
    lent_slot,
    w_first,
    bias_first,
    w_second,
    bias_second,
    w_third,
    bias_third,
):
    count, levels, rows, lon = fields.shape
    groups = lax.axis_size("lev")
    bands = lax.axis_size("lat")
    half = jnp.float16
    f32 = jnp.float32

    near_pairs = [(i, i ^ 1) for i in range(bands) if i ^ 1 < bands]
    far_pairs = [(i, i + 1 if i % 2 else i - 1) for i in range(bands)]
    far_pairs = [(i, j) for i, j in far_pairs if 0 <= j < bands]
    edges = edge_rows(fields)
    far = lax.ppermute((edges[1] * SCALE).astype(half), "lat", far_pairs)
    near = lax.ppermute((edges[0] * SCALE).astype(half), "lat", near_pairs)

    def swap(message):
        sent = [(message[step] * SCALE).astype(half) for step in range(1, groups)]
        return [exchange(value, step + 1, groups) for step, value in enumerate(sent)]

    def received(message, values, unit):
        taken = [message[0]] + [value.astype(f32) * unit for value in values]
        return [taken[step] for step in order]

    local = (fields, courant_lon, courant_lat, displacement, edges, groups)
    network = (
        own_slot, lent_slot, w_first, bias_first.reshape(1, -1), w_second, bias_second.reshape(1, -1),
        w_third, bias_third.reshape(1, -1),
    )
    (inner,) = local_rows(True, *local)
    inner_moved = swap(inner)
    outer = local_rows(False, *local)
    near_message = near_finish(*outer, near.astype(f32) * (1.0 / SCALE), groups)
    message, unit = far_finish(*outer, far.astype(f32) * (1.0 / SCALE), near_message, groups)
    moved = swap(message)
    blocks = tuple((row, row) for row in range(1, rows - 1))
    order = [0, *range(1, min(groups, 2)), *range(groups - 1, 1, -1)]
    sets = (received(inner, inner_moved, unit[0:1, :]),)
    result, unit = physics(sets, order, network, rows, blocks, count, levels)
    sets = (received(message, moved, unit[0:1, :]),)
    return physics(sets, order, network, rows, ((rows - 1, 0), (0, rows - 1)), count, levels, result)[0]


def solution(mesh):
    in_specs = (
        P(None, "lev", "lat", None),
        P("lev", "lat", None),
        P("lev", "lat", None),
        P("lev", "lat", None),
        P("lev", "lat", None),
        P("lev", "lat", None),
        P(),
        P(),
        P(),
        P(),
        P(),
        P(),
    )
    out_specs = P(None, "lat", "lev")
    return jax.shard_map(body, mesh=mesh, in_specs=in_specs, out_specs=out_specs, check_vma=False)
```

```python
import functools

import jax
import jax.numpy as jnp
from jax import lax
from jax.experimental import pallas as pl
from jax.experimental.pallas import tpu as pltpu
from jax.sharding import PartitionSpec as P

LANES = 128
SCALE = 4096.0
SETTLE = 0.87
MEGA = 1024 * 1024
VMEM = pl.BlockSpec(memory_space=pltpu.VMEM)
ANY = pl.BlockSpec(memory_space=pl.ANY)


def place(me, other, count):
    if count & (count - 1) == 0:
        return lax.bitwise_xor(me, other)
    return lax.rem(other - me + count, count)


def source(me, step, count):
    if count & (count - 1) == 0:
        return lax.bitwise_xor(me, step)
    return lax.rem(me - step + count, count)


def exchange(value, step, count):
    power = count & (count - 1) == 0
    return lax.ppermute(value, "lev", [(i, i ^ step if power else (i + step) % count) for i in range(count)])


def params(mega=16):
    return pltpu.CompilerParams(vmem_limit_bytes=mega * MEGA)


def cost(flops, moved):
    return pl.CostEstimate(flops=flops, bytes_accessed=moved, transcendentals=0)


def edge_kernel(fields, out):
    odd = lax.rem(lax.axis_index("lat"), 2)
    out[1 - odd] = fields[:, :, 0, :]
    out[odd] = fields[:, :, fields.shape[2] - 1, :]


def edge_rows(fields):
    count, levels, _, lon = fields.shape
    return pl.pallas_call(
        edge_kernel,
        in_specs=[VMEM],
        out_specs=VMEM,
        out_shape=jax.ShapeDtypeStruct((2, count, levels, lon), fields.dtype),
        compiler_params=params(),
        name="edge_rows",
    )(fields)


def message_height(rows, count, levels):
    return rows * count * levels + -(-rows * count // 8) * 8


def settled(value):
    near = value.astype(jnp.bfloat16).astype(jnp.float32)
    return near + SETTLE * (value - near)


def store_message(message, index, rows, field, count, advected, share, groups, me):
    levels = advected.shape[0]
    flux = share * advected
    depth = lax.broadcasted_iota(jnp.int32, flux.shape, 0)
    above = jnp.where(depth == 0, 0.0, pltpu.roll(flux, 1, 0))
    remapped = settled(advected - flux + above)
    base = (index * count + field) * levels
    row = rows * count * levels + index * count + field
    for group in range(groups):
        where = place(me, group, groups)
        lanes = slice(group * LANES, (group + 1) * LANES)
        message[where, base : base + levels, :] = remapped[:, lanes]
        message[where, row : row + 1, :] = flux[levels - 1 :, lanes]


def moved_share(displacement, row, me, groups):
    share = displacement[:, row, :]
    depth = lax.broadcasted_iota(jnp.int32, share.shape, 0)
    bottom = jnp.logical_and(depth == share.shape[0] - 1, me == groups - 1)
    return jnp.where(bottom, 0.0, share)


def winds(courant):
    return jnp.maximum(courant, 0.0), jnp.minimum(courant, 0.0)


def along_row(here, east_wind, west_wind):
    lon = here.shape[-1]
    result = here - east_wind * (here - pltpu.roll(here, 1, 1))
    return result - west_wind * (pltpu.roll(here, lon - 1, 1) - here)


def local_kernel(groups, inner, fields, along_lon, along_lat, displacement, edges, *outs):
    count, _, rows, _ = fields.shape
    me = lax.axis_index("lev")
    odd = lax.rem(lax.axis_index("lat"), 2)

    def line(row, field):
        return edges[odd if row else 1 - odd, field] if row in (0, rows - 1) else fields[field, :, row, :]

    for row in range(1, rows - 1) if inner else (0, rows - 1):
        east_wind, west_wind = winds(along_lon[:, row, :])
        south_wind, north_wind = winds(along_lat[:, row, :])
        moved = moved_share(displacement, row, me, groups)
        index = int(row > 0)
        if not inner:
            outs[1][index] = -north_wind if row else south_wind
            outs[2][index] = moved
        for field in range(count):
            here = line(row, field)
            north = line(row - 1, field) if row else 0.0
            south = line(row + 1, field) if row < rows - 1 else 0.0
            result = along_row(here, east_wind, west_wind)
            result = result - south_wind * (here - north)
            result = result - north_wind * (south - here)
            if inner:
                store_message(outs[0], row - 1, rows - 2, field, count, result, moved, groups, me)
            else:
                outs[0][index, field] = result


def local_rows(inner, fields, along_lon, along_lat, displacement, edges, groups):
    count, levels, rows, lon = fields.shape
    f32 = jnp.float32
    shapes = [
        jax.ShapeDtypeStruct((2, count, levels, lon), f32),
        jax.ShapeDtypeStruct((2, levels, lon), f32),
        jax.ShapeDtypeStruct((2, levels, lon), f32),
    ]
    if inner:
        shapes = [jax.ShapeDtypeStruct((groups, message_height(rows - 2, count, levels), LANES), f32)]
    return pl.pallas_call(
        functools.partial(local_kernel, groups, inner),
        in_specs=[VMEM] * 5,
        out_specs=[VMEM] * len(shapes),
        out_shape=shapes,
        compiler_params=params(),
        cost_estimate=cost(1_000_000_000, 3_000_000),
        name="inner_rows" if inner else "outer_rows",
    )(fields, along_lon, along_lat, displacement, edges)


def finish_row(groups, far, partial, weight, share, halo, message):
    count = partial.shape[1]
    me = lax.axis_index("lev")
    odd = lax.rem(lax.axis_index("lat"), 2)
    index = odd if far else 1 - odd
    wind, moved = weight[index], share[index]
    for field in range(count):
        advected = partial[index, field] + wind * halo[field]
        store_message(message, 0, 1, field, count, advected, moved, groups, me)


def near_kernel(groups, partial, weight, share, halo, message):
    finish_row(groups, False, partial, weight, share, halo, message)


def far_kernel(groups, partial, weight, share, halo, _, message, unit):
    unit[...] = jnp.full(unit.shape, 1.0 / SCALE, jnp.float32)
    finish_row(groups, True, partial, weight, share, halo, message)


def near_finish(partial, weight, share, halo, groups):
    _, count, levels, _ = partial.shape
    return pl.pallas_call(
        functools.partial(near_kernel, groups),
        in_specs=[VMEM] * 4,
        out_specs=VMEM,
        out_shape=jax.ShapeDtypeStruct((groups, message_height(1, count, levels), LANES), jnp.float32),
        compiler_params=params(),
        name="near_finish",
    )(partial, weight, share, halo)


def far_finish(partial, weight, share, halo, near, groups):
    _, count, levels, _ = partial.shape
    f32 = jnp.float32
    return pl.pallas_call(
        functools.partial(far_kernel, groups),
        in_specs=[VMEM] * 4 + [ANY],
        out_specs=[VMEM] * 2,
        out_shape=[
            jax.ShapeDtypeStruct((groups, message_height(1, count, levels), LANES), f32),
            jax.ShapeDtypeStruct((8, LANES), f32),
        ],
        compiler_params=params(),
        name="far_finish",
    )(partial, weight, share, halo, near)


def silu(value):
    half = 0.5 * value
    return half + half * jnp.tanh(half)


def layer(value, weight, bias, act):
    width = weight.shape[1]
    parts = []
    for start in range(0, width, 256):
        stop = min(start + 256, width)
        total = jnp.dot(value, weight[:, start:stop], preferred_element_type=jnp.float32)
        parts.append(act(total + bias[:, start:stop]).astype(jnp.bfloat16))
    return jnp.concatenate(parts, axis=1)


def active(own, lent, row):
    hits = jnp.logical_or(own[0] == row, lent[0] == row)
    return jnp.max(jnp.where(hits, 1.0, 0.0), axis=1, keepdims=True)


def physics_kernel(groups, order, helds, blocks, count, levels, aliased, *refs):
    sets = [refs[index * groups : (index + 1) * groups] for index in range(len(helds))]
    refs = refs[len(helds) * groups :]
    own, lent, first, bias_first, second, bias_second, third, bias_third = refs[:8]
    outs = refs[8 + aliased :]
    out, columns, carried, staged, sem = outs[0], *outs[-4:]
    if not aliased:
        outs[1][...] = jnp.full(outs[1].shape, 1.0 / SCALE, jnp.float32)
    me = lax.axis_index("lev")
    odd = lax.rem(lax.axis_index("lat"), 2)
    depth = groups * levels
    many = len(blocks)
    at = 0
    for parts, held in zip(sets, helds):
        tall = held * count * levels
        for step, part in zip(order, parts):
            level = source(me, step, groups)
            for index in range(held):
                for field in range(count):
                    start = pl.multiple_of(field * depth + level * levels, levels)
                    base = (index * count + field) * levels
                    columns[at + index, pl.ds(start, levels), :] = part[base : base + levels, :]
                low = tall + index * count
                carried[level, (at + index) * count : (at + index + 1) * count, :] = part[low : low + count, :]
        at += held
    for index in range(many):
        for field in range(count):
            for level in range(1, groups):
                row = field * depth + level * levels
                line = index * count + field
                columns[index, row : row + 1, :] += carried[level - 1, line : line + 1, :]
    value = jnp.concatenate([columns[index].astype(jnp.bfloat16) for index in range(many)], axis=1).T
    hidden = layer(value, first, bias_first, silu)
    hidden = layer(hidden, second, bias_second, silu)
    tendency = layer(hidden, third, bias_third, lambda v: v)

    def send(index, row):
        return pltpu.make_async_copy(staged.at[index], out.at[:, row, :], sem.at[index])

    for index, block in enumerate(blocks):
        part = tendency[index * LANES : (index + 1) * LANES, :].T.astype(jnp.float32)
        row = block[0] if block[0] == block[1] else jnp.where(odd == 1, block[1], block[0])
        staged[index] = columns[index] + jnp.where(active(own, lent, row) > 0.0, part, 0.0)
        if block[0] == block[1]:
            send(index, row).start()
            continue
        for parity in range(2):

            @pl.when(odd == parity)
            def _():
                send(index, block[parity]).start()

    for index, block in enumerate(blocks):
        send(index, block[0]).wait()


def physics(sets, order, network, rows, blocks, count, levels, result=None):
    groups = len(sets[0])
    many = len(blocks)
    width = count * groups * levels
    f32 = jnp.float32
    aliased = int(result is not None)
    unit = jax.ShapeDtypeStruct((8, LANES), f32)
    helds = [parts[0].shape[0] // (count * levels) for parts in sets]
    operands = [part for parts in sets for part in parts] + list(network)
    specs = [VMEM] * len(operands)
    if aliased:
        operands.append(result)
        specs.append(ANY)
    return pl.pallas_call(
        functools.partial(physics_kernel, groups, order, helds, blocks, count, levels, aliased),
        in_specs=specs,
        out_specs=[ANY] + [VMEM] * (1 - aliased),
        out_shape=[jax.ShapeDtypeStruct((width, rows, LANES), f32)] + [unit] * (1 - aliased),
        scratch_shapes=[
            pltpu.VMEM((many, width, LANES), f32),
            pltpu.VMEM((groups, -(-many * count // 8) * 8, LANES), f32),
            pltpu.VMEM((many, width, LANES), f32),
            pltpu.SemaphoreType.DMA((many,)),
        ],
        input_output_aliases={len(operands) - 1: 0} if aliased else {},
        compiler_params=params(),
        cost_estimate=cost(20_000_000_000, 5_000_000),
        name="physics",
    )(*operands)


def body(
    fields,
    courant_lon,
    courant_lat,
    displacement,
    own_slot,
    lent_slot,
    w_first,
    bias_first,
    w_second,
    bias_second,
    w_third,
    bias_third,
):
    count, levels, rows, lon = fields.shape
    groups = lax.axis_size("lev")
    bands = lax.axis_size("lat")
    half = jnp.float16
    f32 = jnp.float32

    near_pairs = [(i, i ^ 1) for i in range(bands) if i ^ 1 < bands]
    far_pairs = [(i, i + 1 if i % 2 else i - 1) for i in range(bands)]
    far_pairs = [(i, j) for i, j in far_pairs if 0 <= j < bands]
    edges = edge_rows(fields)
    far = lax.ppermute((edges[1] * SCALE).astype(half), "lat", far_pairs)
    near = lax.ppermute((edges[0] * SCALE).astype(half), "lat", near_pairs)

    def swap(message):
        sent = [(message[step] * SCALE).astype(half) for step in range(1, groups)]
        return [exchange(value, step + 1, groups) for step, value in enumerate(sent)]

    def received(message, values, unit):
        taken = [message[0]] + [value.astype(f32) * unit for value in values]
        return [taken[step] for step in order]

    local = (fields, courant_lon, courant_lat, displacement, edges, groups)
    network = (
        own_slot, lent_slot, w_first, bias_first.reshape(1, -1), w_second, bias_second.reshape(1, -1),
        w_third, bias_third.reshape(1, -1),
    )
    (inner,) = local_rows(True, *local)
    inner_moved = swap(inner)
    outer = local_rows(False, *local)
    near_message = near_finish(*outer, near.astype(f32) * (1.0 / SCALE), groups)
    far_message, unit = far_finish(*outer, far.astype(f32) * (1.0 / SCALE), near_message, groups)
    tall = near_message.shape[1]
    moved = []
    for step in range(1, groups):
        both = [(message[step] * SCALE).astype(half) for message in (far_message, near_message)]
        moved.append(exchange(jnp.concatenate(both, axis=0), step, groups))

    blocks = tuple((row, row) for row in range(1, rows - 1))
    order = [0, *range(1, min(groups, 2)), *range(groups - 1, 1, -1)]
    sets = (received(inner, inner_moved, unit[0:1, :]),)
    result, unit = physics(sets, order, network, rows, blocks, count, levels)
    order = [0, *range(2, groups), *range(1, min(groups, 2))]
    sets = tuple(
        received(message, [value[at : at + tall] for value in moved], unit[0:1, :])
        for message, at in ((far_message, 0), (near_message, tall))
    )
    return physics(sets, order, network, rows, ((0, rows - 1), (rows - 1, 0)), count, levels, result)[0]


def solution(mesh):
    in_specs = (
        P(None, "lev", "lat", None),
        P("lev", "lat", None),
        P("lev", "lat", None),
        P("lev", "lat", None),
        P("lev", "lat", None),
        P("lev", "lat", None),
        P(),
        P(),
        P(),
        P(),
        P(),
        P(),
    )
    out_specs = P(None, "lat", "lev")
    return jax.shard_map(body, mesh=mesh, in_specs=in_specs, out_specs=out_specs, check_vma=False)
```

```python
import functools

import jax
import jax.numpy as jnp
from jax import lax
from jax.experimental import pallas as pl
from jax.experimental.pallas import tpu as pltpu
from jax.sharding import PartitionSpec as P

LANES = 128
SCALE = 4096.0
SETTLE = 0.87
MEGA = 1024 * 1024
VMEM = pl.BlockSpec(memory_space=pltpu.VMEM)
ANY = pl.BlockSpec(memory_space=pl.ANY)


def place(me, other, count):
    if count & (count - 1) == 0:
        return lax.bitwise_xor(me, other)
    return lax.rem(other - me + count, count)


def source(me, step, count):
    if count & (count - 1) == 0:
        return lax.bitwise_xor(me, step)
    return lax.rem(me - step + count, count)


def exchange(value, step, count):
    power = count & (count - 1) == 0
    return lax.ppermute(value, "lev", [(i, i ^ step if power else (i + step) % count) for i in range(count)])


def params(mega=16):
    return pltpu.CompilerParams(vmem_limit_bytes=mega * MEGA)


def cost(flops, moved):
    return pl.CostEstimate(flops=flops, bytes_accessed=moved, transcendentals=0)


def edge_kernel(fields, out):
    out[0] = fields[:, :, 0, :]
    out[1] = fields[:, :, fields.shape[2] - 1, :]


def edge_rows(fields):
    count, levels, _, lon = fields.shape
    return pl.pallas_call(
        edge_kernel,
        in_specs=[VMEM],
        out_specs=VMEM,
        out_shape=jax.ShapeDtypeStruct((2, count, levels, lon), fields.dtype),
        compiler_params=params(),
        name="edge_rows",
    )(fields)


def message_height(rows, count, levels):
    return rows * count * levels + -(-rows * count // 8) * 8


def settled(value):
    near = value.astype(jnp.bfloat16).astype(jnp.float32)
    return near + SETTLE * (value - near)


def store_message(message, index, rows, field, count, advected, share, groups, me):
    levels = advected.shape[0]
    flux = share * advected
    depth = lax.broadcasted_iota(jnp.int32, flux.shape, 0)
    above = jnp.where(depth == 0, 0.0, pltpu.roll(flux, 1, 0))
    remapped = settled(advected - flux + above)
    base = (index * count + field) * levels
    row = rows * count * levels + index * count + field
    for group in range(groups):
        where = place(me, group, groups)
        lanes = slice(group * LANES, (group + 1) * LANES)
        message[where, base : base + levels, :] = remapped[:, lanes]
        message[where, row : row + 1, :] = flux[levels - 1 :, lanes]


def moved_share(displacement, row, me, groups):
    share = displacement[:, row, :]
    depth = lax.broadcasted_iota(jnp.int32, share.shape, 0)
    bottom = jnp.logical_and(depth == share.shape[0] - 1, me == groups - 1)
    return jnp.where(bottom, 0.0, share)


def winds(courant):
    return jnp.maximum(courant, 0.0), jnp.minimum(courant, 0.0)


def along_row(here, east_wind, west_wind):
    lon = here.shape[-1]
    result = here - east_wind * (here - pltpu.roll(here, 1, 1))
    return result - west_wind * (pltpu.roll(here, lon - 1, 1) - here)


def local_kernel(groups, inner, fields, along_lon, along_lat, displacement, edges, *outs):
    count, _, rows, _ = fields.shape
    me = lax.axis_index("lev")

    def line(row, field):
        return edges[int(row > 0), field] if row in (0, rows - 1) else fields[field, :, row, :]

    for row in range(1, rows - 1) if inner else (0, rows - 1):
        east_wind, west_wind = winds(along_lon[:, row, :])
        south_wind, north_wind = winds(along_lat[:, row, :])
        moved = moved_share(displacement, row, me, groups)
        index = int(row > 0)
        if not inner:
            outs[1][index] = -north_wind if row else south_wind
            outs[2][index] = moved
        for field in range(count):
            here = line(row, field)
            north = line(row - 1, field) if row else 0.0
            south = line(row + 1, field) if row < rows - 1 else 0.0
            result = along_row(here, east_wind, west_wind)
            result = result - south_wind * (here - north)
            result = result - north_wind * (south - here)
            if inner:
                store_message(outs[0], row - 1, rows - 2, field, count, result, moved, groups, me)
            else:
                outs[0][index, field] = result


def local_rows(inner, fields, along_lon, along_lat, displacement, edges, groups):
    count, levels, rows, lon = fields.shape
    f32 = jnp.float32
    shapes = [
        jax.ShapeDtypeStruct((2, count, levels, lon), f32),
        jax.ShapeDtypeStruct((2, levels, lon), f32),
        jax.ShapeDtypeStruct((2, levels, lon), f32),
    ]
    if inner:
        shapes = [jax.ShapeDtypeStruct((groups, message_height(rows - 2, count, levels), LANES), f32)]
    return pl.pallas_call(
        functools.partial(local_kernel, groups, inner),
        in_specs=[VMEM] * 5,
        out_specs=[VMEM] * len(shapes),
        out_shape=shapes,
        compiler_params=params(),
        cost_estimate=cost(1_000_000_000, 3_000_000),
        name="inner_rows" if inner else "outer_rows",
    )(fields, along_lon, along_lat, displacement, edges)


def finish_row(groups, far, rows, partial, weight, share, halo, message):
    count = partial.shape[1]
    me = lax.axis_index("lev")
    odd = lax.rem(lax.axis_index("lat"), 2)
    index = odd if far else 1 - odd
    wind, moved = weight[index], share[index]
    for field in range(count):
        advected = partial[index, field] + wind * halo[field]
        store_message(message, int(far), rows, field, count, advected, moved, groups, me)


def near_kernel(groups, partial, weight, share, halo, message):
    finish_row(groups, False, 1, partial, weight, share, halo, message)


def far_kernel(groups, partial, weight, share, halo, near, message, unit):
    count, levels = partial.shape[1:3]
    size = count * levels
    unit[...] = jnp.full(unit.shape, 1.0 / SCALE, jnp.float32)
    message[:, 0:size, :] = near[:, 0:size, :]
    message[:, 2 * size : 2 * size + count, :] = near[:, size : size + count, :]
    finish_row(groups, True, 2, partial, weight, share, halo, message)


def near_finish(partial, weight, share, halo, groups):
    _, count, levels, _ = partial.shape
    return pl.pallas_call(
        functools.partial(near_kernel, groups),
        in_specs=[VMEM] * 4,
        out_specs=VMEM,
        out_shape=jax.ShapeDtypeStruct((groups, message_height(1, count, levels), LANES), jnp.float32),
        compiler_params=params(),
        name="near_finish",
    )(partial, weight, share, halo)


def far_finish(partial, weight, share, halo, near, groups):
    _, count, levels, _ = partial.shape
    f32 = jnp.float32
    return pl.pallas_call(
        functools.partial(far_kernel, groups),
        in_specs=[VMEM] * 5,
        out_specs=[VMEM] * 2,
        out_shape=[
            jax.ShapeDtypeStruct((groups, message_height(2, count, levels), LANES), f32),
            jax.ShapeDtypeStruct((8, LANES), f32),
        ],
        compiler_params=params(),
        name="far_finish",
    )(partial, weight, share, halo, near)


def silu(value):
    half = 0.5 * value
    return half + half * jnp.tanh(half)


def layer(value, weight, bias, act):
    width = weight.shape[1]
    parts = []
    for start in range(0, width, 256):
        stop = min(start + 256, width)
        total = jnp.dot(value, weight[:, start:stop], preferred_element_type=jnp.float32)
        parts.append(act(total + bias[:, start:stop]).astype(jnp.bfloat16))
    return jnp.concatenate(parts, axis=1)


def active(own, lent, row):
    hits = jnp.logical_or(own[0] == row, lent[0] == row)
    return jnp.max(jnp.where(hits, 1.0, 0.0), axis=1, keepdims=True)


def physics_kernel(groups, order, helds, blocks, count, levels, aliased, *refs):
    sets = [refs[index * groups : (index + 1) * groups] for index in range(len(helds))]
    refs = refs[len(helds) * groups :]
    own, lent, first, bias_first, second, bias_second, third, bias_third = refs[:8]
    outs = refs[8 + aliased :]
    out, columns, carried, staged, sem = outs[0], *outs[-4:]
    if not aliased:
        outs[1][...] = jnp.full(outs[1].shape, 1.0 / SCALE, jnp.float32)
    me = lax.axis_index("lev")
    odd = lax.rem(lax.axis_index("lat"), 2)
    depth = groups * levels
    many = len(blocks)
    at = 0
    for parts, held in zip(sets, helds):
        tall = held * count * levels
        for step, part in zip(order, parts):
            level = source(me, step, groups)
            for index in range(held):
                for field in range(count):
                    start = pl.multiple_of(field * depth + level * levels, levels)
                    base = (index * count + field) * levels
                    columns[at + index, pl.ds(start, levels), :] = part[base : base + levels, :]
                low = tall + index * count
                carried[level, (at + index) * count : (at + index + 1) * count, :] = part[low : low + count, :]
        at += held
    for index in range(many):
        for field in range(count):
            for level in range(1, groups):
                row = field * depth + level * levels
                line = index * count + field
                columns[index, row : row + 1, :] += carried[level - 1, line : line + 1, :]
    value = jnp.concatenate([columns[index].astype(jnp.bfloat16).T for index in range(many)], axis=0)
    hidden = layer(value, first, bias_first, silu)
    hidden = layer(hidden, second, bias_second, silu)
    tendency = layer(hidden, third, bias_third, lambda v: v)

    def send(index, row):
        return pltpu.make_async_copy(staged.at[index], out.at[:, row, :], sem.at[index])

    for index, block in enumerate(blocks):
        part = tendency[index * LANES : (index + 1) * LANES, :].T.astype(jnp.float32)
        row = block[0] if block[0] == block[1] else jnp.where(odd == 1, block[1], block[0])
        staged[index] = columns[index] + jnp.where(active(own, lent, row) > 0.0, part, 0.0)
        if block[0] == block[1]:
            send(index, row).start()
            continue
        for parity in range(2):

            @pl.when(odd == parity)
            def _():
                send(index, block[parity]).start()

    for index, block in enumerate(blocks):
        send(index, block[0]).wait()


def physics(sets, order, network, rows, blocks, count, levels, result=None):
    groups = len(sets[0])
    many = len(blocks)
    width = count * groups * levels
    f32 = jnp.float32
    aliased = int(result is not None)
    unit = jax.ShapeDtypeStruct((8, LANES), f32)
    helds = [parts[0].shape[0] // (count * levels) for parts in sets]
    operands = [part for parts in sets for part in parts] + list(network)
    specs = [VMEM] * len(operands)
    if aliased:
        operands.append(result)
        specs.append(ANY)
    return pl.pallas_call(
        functools.partial(physics_kernel, groups, order, helds, blocks, count, levels, aliased),
        in_specs=specs,
        out_specs=[ANY] + [VMEM] * (1 - aliased),
        out_shape=[jax.ShapeDtypeStruct((width, rows, LANES), f32)] + [unit] * (1 - aliased),
        scratch_shapes=[
            pltpu.VMEM((many, width, LANES), f32),
            pltpu.VMEM((groups, -(-many * count // 8) * 8, LANES), f32),
            pltpu.VMEM((many, width, LANES), f32),
            pltpu.SemaphoreType.DMA((many,)),
        ],
        input_output_aliases={len(operands) - 1: 0} if aliased else {},
        compiler_params=params(),
        cost_estimate=cost(20_000_000_000, 5_000_000),
        name="physics",
    )(*operands)


def body(
    fields,
    courant_lon,
    courant_lat,
    displacement,
    own_slot,
    lent_slot,
    w_first,
    bias_first,
    w_second,
    bias_second,
    w_third,
    bias_third,
):
    count, levels, rows, lon = fields.shape
    groups = lax.axis_size("lev")
    bands = lax.axis_size("lat")
    even = lax.axis_index("lat") % 2 == 0
    half = jnp.float16
    f32 = jnp.float32

    near_pairs = [(i, i ^ 1) for i in range(bands) if i ^ 1 < bands]
    far_pairs = [(i, i + 1 if i % 2 else i - 1) for i in range(bands)]
    far_pairs = [(i, j) for i, j in far_pairs if 0 <= j < bands]
    edges = edge_rows(fields)
    far = lax.ppermute((jnp.where(even, edges[0], edges[1]) * SCALE).astype(half), "lat", far_pairs)
    near = lax.ppermute((jnp.where(even, edges[1], edges[0]) * SCALE).astype(half), "lat", near_pairs)

    def swap(message):
        sent = [(message[step] * SCALE).astype(half) for step in range(1, groups)]
        return [exchange(value, step + 1, groups) for step, value in enumerate(sent)]

    def received(message, values, unit):
        taken = [message[0]] + [value.astype(f32) * unit for value in values]
        return [taken[step] for step in order]

    local = (fields, courant_lon, courant_lat, displacement, edges, groups)
    network = (
        own_slot, lent_slot, w_first, bias_first.reshape(1, -1), w_second, bias_second.reshape(1, -1),
        w_third, bias_third.reshape(1, -1),
    )
    (inner,) = local_rows(True, *local)
    inner_moved = swap(inner)
    outer = local_rows(False, *local)
    near_message = near_finish(*outer, near.astype(f32) * (1.0 / SCALE), groups)
    message, unit = far_finish(*outer, far.astype(f32) * (1.0 / SCALE), near_message, groups)
    moved = swap(message)
    blocks = tuple((row, row) for row in range(1, rows - 1))
    order = [0, *range(1, min(groups, 2)), *range(groups - 1, 1, -1)]
    sets = (received(inner, inner_moved, unit[0:1, :]),)
    result, unit = physics(sets, order, network, rows, blocks, count, levels)
    sets = (received(message, moved, unit[0:1, :]),)
    return physics(sets, order, network, rows, ((rows - 1, 0), (0, rows - 1)), count, levels, result)[0]


def solution(mesh):
    in_specs = (
        P(None, "lev", "lat", None),
        P("lev", "lat", None),
        P("lev", "lat", None),
        P("lev", "lat", None),
        P("lev", "lat", None),
        P("lev", "lat", None),
        P(),
        P(),
        P(),
        P(),
        P(),
        P(),
    )
    out_specs = P(None, "lat", "lev")
    return jax.shard_map(body, mesh=mesh, in_specs=in_specs, out_specs=out_specs, check_vma=False)
```
